128 devices in a mesh: rep: 2 (over x_lo), ep: 64 (over y, z, x_hi, core).
Axes of the slice: x: 4 (x_hi: 2, x_lo: 2; x = x_hi * 2 + x_lo), y: 4, z: 4, core: 2. Of those that a mesh axis runs over, the one named last changes fastest.
Arguments:
- query_nope: bfloat16 [2048, 8192], P(('rep', 'ep')), may hold values from -6 to 6
- query_rope: bfloat16 [2048, 4096], P(('rep', 'ep')), may hold values from -150 to 150
- query_compressed: bfloat16 [2048, 1536], P(('rep', 'ep')), may hold values from -6 to 6
- kv_cache: bfloat16 [2048, 192, 576], P(('rep', 'ep')), may hold values from -8 to 8
- cache_lengths: int32 [2048], P(('rep', 'ep')), may hold values from 2 to 192
- key_base: bfloat16 [64, 128, 512], P('rep'), may hold values from -0.25 to 0.25
- query_down: bfloat16 [2, 1536, 64], P('rep'), may hold values from -0.15625 to 0.15625
- query_rise: bfloat16 [2, 64, 8192], P('rep'), may hold values from -0.75 to 0.75
- key_down: bfloat16 [2, 64, 512], P('rep'), may hold values from -0.25 to 0.25
- key_rise: bfloat16 [2, 64, 8192], P('rep'), may hold values from -0.75 to 0.75
- moe_input: bfloat16 [2048, 3584], P(('rep', 'ep')), may hold values from -6 to 6
- expert_ids: int32 [2048, 8], P(('rep', 'ep')), may hold values from 0 to 127, all different within a row; in each aligned block of 16 rows (0 to 15, 16 to 31, ...) at most 3 rows name the same one
- route_weights: float32 [2048, 8], P(('rep', 'ep')), may hold values from 0.1 to 1
- expert_gate_up: bfloat16 [128, 3584, 2048], P(('rep', 'ep')), may hold values from -0.09375 to 0.09375
Outputs:
- attended: bfloat16 [2048, 32768], P(('rep', 'ep'))
- expert_hidden: bfloat16 [2048, 8192], P(('rep', 'ep'))
The draws below stay inside these ranges and needn't reach their ends.
Inputs may be any that keep to these rules, and one draw needn't show every extreme that they name: `expert_ids`: A row names 8 different experts; among the rows of one device no expert is named by more than 3 rows, a bound that some block reaches.
All inputs are finite; a program needn't handle non-finite values.
Results may differ from the reference program's by a relative error of at most 0.0077.
Values may be sent and summed in bfloat16 or wider, within the bound.
No kernel may reach another device: no remote copies, remote signals or barrier semaphores. Data moves between devices by JAX's collectives and lax.ppermute only.
A program may use at most 128 MiB of HBM per device.

```python
import math
import jax
import jax.numpy as jnp
import numpy as np
from jax import lax

HEADS = 64
NOPE = 128
ROPE = 64
LATENT = 512
QLORA = 1536
RANK = 64
D = 3584
EH = 1024
TOPK = 8
ROWS = 16
LEN = 192
ROWS_ALL = 2048
EXPERTS = 128
CAP = 3
N_REP = 2
N_EP = 64


def draw_kv_cache(key, part):
    key = jax.random.fold_in(key, 2)
    cache = jnp.clip(jax.random.normal(key, (ROWS_ALL, LEN, LATENT + ROPE), jnp.float32), -5.0, 5.0)
    return cache.astype(jnp.bfloat16)


def draw_query_rope(key, part):
    key = jax.random.fold_in(key, 3)
    values = jnp.clip(jax.random.normal(key, (ROWS_ALL, HEADS, ROPE), jnp.float32), -5.0, 5.0)
    return values.reshape(ROWS_ALL, HEADS * ROPE).astype(jnp.bfloat16)


def draw_cache_lengths(key, part):
    key = jax.random.fold_in(key, 5)
    key_len, key_full, key_short = jax.random.split(key, 3)
    lengths = jax.random.randint(key_len, (ROWS_ALL,), 2, LEN + 1)
    full_row = jax.random.randint(key_full, (), 0, ROWS_ALL)
    short_row = (full_row + 1 + jax.random.randint(key_short, (), 0, ROWS_ALL - 1)) % ROWS_ALL
    row_numbers = jnp.arange(ROWS_ALL)
    lengths = jnp.where(row_numbers == full_row, LEN, lengths)
    lengths = jnp.where(row_numbers == short_row, 2, lengths)
    return lengths.astype(jnp.int32)


def steps_of(rng, extent, shards, smallest, top_value):
    loudness, own = 1.0, jax.random.fold_in(rng, 6)
    for axis_at, blocks in shards:
        steps = jnp.exp(jax.random.uniform(jax.random.fold_in(own, axis_at), (blocks,), jnp.float32, smallest / len(shards), top_value / len(shards)))
        loudness = loudness * jnp.repeat(steps, extent[axis_at] // blocks).reshape([-1 if axis == axis_at else 1 for axis in range(len(extent))])
    return loudness


def deal_out(stream_key, own, number, rows, amount, top, reach, lean):
    sequence = jax.random.permutation(stream_key, amount)
    packed, ordinary = shares(amount, rows * top, reach, lean, True), shares(amount, rows * top, reach, lean, False)
    places = jnp.arange(amount)

    def named(tallies, turn):
        used = int((tallies > 0).sum())
        fixed = max(1, used // 4)
        moved = fixed + (places - fixed + turn * (used - fixed)) % max(1, amount - fixed)
        return jnp.zeros((amount,), jnp.int32).at[sequence[jnp.where(places < fixed, places, moved)]].set(jnp.asarray(tallies, jnp.int32))

    tallies = jnp.where(number % 4 == 0, named(packed, number // 4), named(ordinary, number - number // 4 - 1))
    mixed = jax.random.permutation(jax.random.fold_in(own, 3), amount)
    giver, sink = mixed[0:amount // 2 * 2:2], mixed[1:amount // 2 * 2:2]
    margin = jnp.minimum(tallies[giver] - 1, reach - tallies[sink]) // 2
    margin = jnp.where((giver == sequence[0]) | (sink == sequence[0]) | (tallies[sink] == 0), 0, jnp.maximum(margin, 0))
    moved = jax.random.randint(jax.random.fold_in(own, 4), (amount // 2,), 0, 1 << 20) % (margin + 1)
    tallies = tallies.at[giver].add(-moved).at[sink].add(moved)
    items = jnp.searchsorted(jnp.cumsum(tallies), jnp.arange(rows * top), side="right").astype(jnp.int32)
    table = items.reshape(top, rows).T
    table = table[jax.random.permutation(jax.random.fold_in(own, 1), rows)]
    turn = jax.random.randint(jax.random.fold_in(own, 2), (rows, 1), 0, top)
    return jnp.take_along_axis(table, (jnp.arange(top)[None, :] + turn) % top, axis=1)


def shares(count, total, most, slope, full):
    weights = [(1 << 20) // math.isqrt(standing ** slope) + 1 for standing in range(1, count + 1)]
    largest = most if full else min(most, max(-(-total // count), total * weights[0] // sum(weights)))
    least = 1 if total - largest >= count - 1 else 0
    given, surplus = [largest] + [least] * (count - 1), total - largest - least * (count - 1)
    while surplus > 0:
        movable = [i for i in range(1, count) if given[i] < largest] or [i for i in range(1, count) if given[i] < most]
        pool, remaining = sum([weights[i] for i in movable]), surplus
        for i in movable:
            addition = min(most - given[i], max(1, remaining * weights[i] // pool), surplus)
            given[i] = given[i] + addition
            surplus = surplus - addition
    return np.array(given)


def scatter_about(key, dims, deviation, bound, cuts=(), held_as=jnp.bfloat16):
    result = deviation * jax.random.normal(key, dims, jnp.float32)
    if cuts:
        result = result * steps_of(key, dims, cuts, -0.22, 0.18)
    return jnp.clip(result, -bound, bound).astype(held_as)


def setup_inputs(seed: int = 0) -> dict:
    streams_of = jax.random.split(jax.random.key(seed), 15)
    query_nope = scatter_about(streams_of[0], (ROWS_ALL, HEADS * NOPE), 1.0, 6.0, ((0, 128),))
    query_rope = draw_query_rope(jax.random.fold_in(streams_of[14], 71), 0)
    query_compressed = scatter_about(streams_of[2], (ROWS_ALL, QLORA), 1.0, 6.0, ((0, 128),))
    kv_cache = draw_kv_cache(jax.random.fold_in(streams_of[14], 71), 0)
    cache_lengths = draw_cache_lengths(jax.random.fold_in(streams_of[14], 71), 0)
    key_base = scatter_about(streams_of[5], (HEADS, NOPE, LATENT), LATENT ** -0.5, 0.25, ((0, 2),))
    query_down = scatter_about(streams_of[6], (N_REP, QLORA, RANK), QLORA ** -0.5, 0.15625, ((0, 2),))
    query_rise = scatter_about(streams_of[7], (N_REP, RANK, HEADS * NOPE), RANK ** -0.5, 0.75, ((0, 2),))
    key_down = scatter_about(streams_of[8], (N_REP, RANK, LATENT), LATENT ** -0.5, 0.25, ((0, 2),))
    key_rise = scatter_about(streams_of[9], (N_REP, RANK, HEADS * NOPE), RANK ** -0.5, 0.75, ((0, 2),))
    moe_input = scatter_about(streams_of[10], (ROWS_ALL, D), 1.0, 6.0, ((0, 128),))
    expert_ids_keys = jax.random.split(jax.random.fold_in(streams_of[11], 1), ROWS_ALL // ROWS)
    expert_ids_turns = jax.random.permutation(jax.random.fold_in(streams_of[11], 3), ROWS_ALL // ROWS)
    expert_ids = jax.vmap(lambda own, number: deal_out(jax.random.fold_in(streams_of[11], 2), own, number, ROWS, EXPERTS, TOPK, CAP, 2))(expert_ids_keys, expert_ids_turns).reshape((ROWS_ALL, TOPK))
    route_weights = jnp.clip(0.1 + 0.9 * jax.random.uniform(streams_of[12], (ROWS_ALL, TOPK), jnp.float32) ** steps_of(streams_of[12], (ROWS_ALL, TOPK), ((0, 128),), -0.2, 0.2), 0.1, 1.0)
    expert_gate_up = scatter_about(streams_of[13], (EXPERTS, D, 2 * EH), D ** -0.5, 0.09375, ((0, 128),))
    return dict(query_nope=query_nope, query_rope=query_rope, query_compressed=query_compressed, kv_cache=kv_cache, cache_lengths=cache_lengths, key_base=key_base, query_down=query_down, query_rise=query_rise, key_down=key_down, key_rise=key_rise, moe_input=moe_input, expert_ids=expert_ids, route_weights=route_weights, expert_gate_up=expert_gate_up)


masked_score = -1e30


def attend_block(operands):
    query_full, kv_block, lengths = operands
    scaling = 1.0 / (NOPE + ROPE) ** 0.5
    scores = jnp.einsum("bhc,btc->bht", query_full.astype(jnp.float32), kv_block.astype(jnp.float32)) * scaling
    positions = lax.broadcasted_iota(jnp.int32, scores.shape, 2)
    valid_mask = positions < lengths.astype(jnp.int32)[:, None, None]
    scores = jnp.where(valid_mask, scores, masked_score)
    highest = jnp.max(scores, axis=2, keepdims=True)
    exponent = jnp.where(valid_mask, jnp.exp(scores - highest), 0.0)
    weights = (exponent / jnp.sum(exponent, axis=2, keepdims=True)).astype(jnp.bfloat16)
    latent = jnp.einsum("bht,btl->bhl", weights.astype(jnp.float32), kv_block[:, :, :LATENT].astype(jnp.float32))
    return latent.astype(jnp.bfloat16)


def reference(query_nope, query_rope, query_compressed, kv_cache, cache_lengths, key_base, query_down, query_rise, key_down, key_rise, moe_input, expert_ids, route_weights, expert_gate_up):
    down_query = query_down[0]
    rise_query = query_rise[0]
    down_key = key_down[0]
    rise_key = key_rise[0]
    query_low = jnp.dot(query_compressed, down_query, preferred_element_type=jnp.float32).astype(jnp.bfloat16)
    query_heads = (query_nope.astype(jnp.float32) + jnp.dot(query_low, rise_query, preferred_element_type=jnp.float32)).astype(jnp.bfloat16)
    query_heads = query_heads.reshape(ROWS_ALL, HEADS, NOPE)
    low_rank = jnp.einsum("rhn,rl->hnl", rise_key.astype(jnp.float32).reshape(RANK, HEADS, NOPE), down_key.astype(jnp.float32), precision=lax.Precision.HIGHEST)
    key_proj = key_base.astype(jnp.float32) + low_rank
    query_latent = jnp.einsum("ihn,hnl->ihl", query_heads.astype(jnp.float32), key_proj, precision=lax.Precision.HIGHEST).astype(jnp.bfloat16)
    query_full = jnp.concatenate([query_latent, query_rope.reshape(ROWS_ALL, HEADS, ROPE)], axis=2)
    blocks = ROWS_ALL // ROWS
    attended = lax.map(attend_block, (query_full.reshape(blocks, ROWS, HEADS, LATENT + ROPE), kv_cache.reshape(blocks, ROWS, LEN, LATENT + ROPE), cache_lengths.reshape(blocks, ROWS)))
    attended = attended.reshape(ROWS_ALL, HEADS * LATENT)

    flat_ids = expert_ids.reshape(-1).astype(jnp.int32)
    entries = ROWS_ALL * TOPK
    slot_limit = N_REP * N_EP * CAP
    sorted_entries = jnp.argsort(flat_ids, stable=True).astype(jnp.int32)
    padded = jnp.concatenate([sorted_entries, jnp.full((slot_limit,), entries, jnp.int32)])
    counts = jnp.sum((flat_ids[:, None] == jnp.arange(EXPERTS, dtype=jnp.int32)[None, :]).astype(jnp.int32), axis=0)
    starts = (jnp.cumsum(counts) - counts).astype(jnp.int32)

    def one_expert(expert):
        first_slot = starts[expert]
        members = lax.dynamic_slice_in_dim(padded, first_slot, slot_limit)
        in_use = jnp.arange(slot_limit, dtype=jnp.int32) < counts[expert]
        chosen = jnp.where(in_use, members, 0)
        expert_rows = moe_input[chosen // TOPK]
        gate_up = jnp.dot(expert_rows, expert_gate_up[expert], preferred_element_type=jnp.float32)
        activation = (jax.nn.silu(gate_up[:, :EH]) * gate_up[:, EH:]).astype(jnp.bfloat16)
        return activation, jnp.where(in_use, members, entries).astype(jnp.int32)

    activations, targets = lax.map(one_expert, jnp.arange(EXPERTS, dtype=jnp.int32))
    gathered = jnp.zeros((entries, EH), jnp.bfloat16).at[targets.reshape(-1)].set(activations.reshape(-1, EH), mode="drop")
    scaled = route_weights.reshape(-1, 1) * gathered.astype(jnp.float32)
    expert_hidden = scaled.astype(jnp.bfloat16).reshape(ROWS_ALL, TOPK * EH)
    return attended, expert_hidden
```

```python
import functools

import jax
import jax.numpy as jnp
from jax import lax
from jax.experimental import pallas as pl
from jax.experimental.pallas import tpu as pltpu
from jax.sharding import PartitionSpec as P

HEADS = 64
NOPE = 128
ROPE = 64
LATENT = 512
RANK = 64
QLORA = 1536
D = 3584
EH = 1024
TOPK = 8
ROWS = 16
LEN = 192
EXPERTS = 128
HALF = HEADS // 2
HCOLS = HALF * NOPE
GROUP = 8
PATH_COLS = HCOLS // 2
QUARTER = RANK // 4
COMP_AT = PATH_COLS
RISE_Q_AT = COMP_AT + QLORA
RISE_K_AT = RISE_Q_AT + HCOLS
DOWN_K_AT = RISE_K_AT + HCOLS
DOWN_Q_AT = DOWN_K_AT + LATENT
PAYLOAD = DOWN_Q_AT + QLORA
AXES = ("rep", "ep")
MIB = 1 << 20

f32 = jnp.float32
bf16 = jnp.bfloat16


def contract(a, b, dims):
    return lax.dot_general(a, b, (dims, ((), ())), preferred_element_type=f32)


def vmem():
    return pl.BlockSpec(memory_space=pltpu.VMEM)


def in_hbm(x):
    return pltpu.with_memory_space_constraint(x, pltpu.HBM)


def params(mib, **more):
    return pltpu.CompilerParams(vmem_limit_bytes=mib * MIB, **more)


def cost(flops, moved, exps=0):
    return pl.CostEstimate(flops=flops, bytes_accessed=moved, transcendentals=exps)


def named_and_rank(ids, slots, shift):
    expert = lax.broadcasted_iota(jnp.int32, (slots, ROWS), 0)
    if shift:
        expert = lax.shift_right_logical(expert, shift)
    named = jnp.zeros((slots, ROWS), f32)
    for c in range(TOPK):
        named = jnp.where(ids[c : c + 1, :] == expert, 1.0, named)
    above = lax.broadcasted_iota(jnp.int32, (ROWS, ROWS), 0) < lax.broadcasted_iota(
        jnp.int32, (ROWS, ROWS), 1
    )
    rank = contract(named.astype(bf16), above.astype(bf16), ((1,), (0,)))
    return named, rank


def slot_masks(ids):
    named, rank = named_and_rank(ids, 2 * EXPERTS, 1)
    slot = lax.broadcasted_iota(jnp.int32, (2 * EXPERTS, ROWS), 0) & 1
    mask_a = jnp.where(rank == slot.astype(f32), named, 0.0)
    named, rank = named_and_rank(ids, EXPERTS, 0)
    mask_b = jnp.where(rank == 2.0, named, 0.0)
    return mask_a, mask_b


PIECE = 512
PIECES = D // PIECE
TAKEN = (1, 1, 2, 2, 1)
SPAN = PIECE + PIECE // 2
TILE = 256
TILES = EH // TILE
STRIDE = TILE + TILE // 2


def payload_kernel(place_ref, *refs):
    widths = (PATH_COLS, QLORA, HCOLS, HCOLS, LATENT, QLORA)
    for path in range(2):
        at = 0
        for k, width in enumerate(widths):
            refs[12 + path][:, at : at + width] = refs[6 * path + k][...]
            at += width


def payloads(place, nope, comp, rise_q, rise_k, down_k, down_q):
    specs = []
    for path in range(2):
        quarter = lambda column, path=path: lambda _, p: (p[1] * 2 + path, column)
        specs += [
            pl.BlockSpec((ROWS, PATH_COLS), lambda _, p, path=path: (0, (1 - p[0]) * 2 + path)),
            pl.BlockSpec((ROWS, QLORA), lambda _, p: (0, 0)),
            pl.BlockSpec((QUARTER, HCOLS), quarter(1)),
            pl.BlockSpec((QUARTER, HCOLS), quarter(1)),
            pl.BlockSpec((QUARTER, LATENT), quarter(0)),
            pl.BlockSpec((QUARTER, QLORA), quarter(0)),
        ]
    given = tuple(map(in_hbm, (nope, comp, rise_q, rise_k, down_k, down_q)))
    return pl.pallas_call(
        payload_kernel,
        out_shape=(
            jax.ShapeDtypeStruct((ROWS, PAYLOAD), bf16),
            jax.ShapeDtypeStruct((ROWS, PAYLOAD), bf16),
        ),
        grid_spec=pltpu.PrefetchScalarGridSpec(
            num_scalar_prefetch=1,
            grid=(1,),
            in_specs=specs,
            out_specs=(pl.BlockSpec((ROWS, PAYLOAD), lambda _, p: (0, 0)),) * 2,
        ),
        compiler_params=params(16),
        cost_estimate=cost(1 << 10, 1 << 20),
        name="payloads",
    )(place, *given, *given)


def pack_kernel(ids_ref, x_ref, o_ref, packed_ref, sent):
    mask_a, mask_b = slot_masks(ids_ref[...])
    mask_a, mask_b = mask_a.astype(bf16), mask_b.astype(bf16)
    copies = []
    for g in range(PIECES):
        x = x_ref[:, g * PIECE : (g + 1) * PIECE]
        at = g * SPAN
        rows = contract(mask_a, x, ((1,), (0,))).astype(bf16)
        packed_ref[:, :, at : at + PIECE] = rows.reshape(EXPERTS, 2, PIECE)
        rows = contract(mask_b, x, ((1,), (0,))).astype(bf16)
        packed_ref[:, :, at + PIECE : at + SPAN] = rows.reshape(EXPERTS, 2, PIECE // 2)
        lanes = pl.ds(at, SPAN)
        copy = pltpu.make_async_copy(
            packed_ref.at[:, :, lanes], o_ref.at[:, :, lanes], sent.at[g]
        )
        copy.start()
        copies.append(copy)
    for copy in copies:
        copy.wait()


def pack(ids, x):
    shape = (EXPERTS, 2, PIECES * SPAN)
    return pl.pallas_call(
        pack_kernel,
        out_shape=pltpu.HBM(shape, bf16),
        in_specs=[vmem(), vmem()],
        out_specs=pl.BlockSpec(memory_space=pltpu.HBM),
        scratch_shapes=[pltpu.VMEM(shape, bf16), pltpu.SemaphoreType.DMA((PIECES,))],
        compiler_params=params(16),
        cost_estimate=cost(2 * 384 * ROWS * D, 3 * MIB),
        name="pack_rows",
    )(ids, x)


def expert_kernel(x_ref, w_ref, o_ref, xs_ref, held_ref, sum_ref, came):
    rows, wide = 3 * EXPERTS, 2 * TILE
    copies = []
    for g in range(PIECES):
        part = pl.ds(g * PIECE, PIECE)
        copy = pltpu.make_async_copy(w_ref.at[0, part, :], held_ref.at[part, :], came.at[g])
        copy.start()
        copies.append(copy)
    for g in range(PIECES):
        at, to = g * SPAN, slice(g * PIECE, (g + 1) * PIECE)
        xs_ref[: 2 * EXPERTS, to] = x_ref[:, :, at : at + PIECE].reshape(2 * EXPERTS, PIECE)
        xs_ref[2 * EXPERTS :, to] = x_ref[:, :, at + PIECE : at + SPAN].reshape(EXPERTS, PIECE)
    done = 0
    for take in TAKEN[:-1]:
        for g in range(done, done + take):
            copies[g].wait()
        part = slice(done * PIECE, (done + take) * PIECE)
        for n in range(2 * EH // wide):
            to = slice(n * wide, (n + 1) * wide)
            term = contract(xs_ref[:, part], held_ref[part, to], ((1,), (0,)))
            sum_ref[:, to] = term if done == 0 else sum_ref[:, to] + term
        done += take
    for g in range(done, PIECES):
        copies[g].wait()
    part = slice(done * PIECE, D)
    for n in range(TILES):
        both = []
        for k in range(2):
            to = slice(k * EH + n * TILE, k * EH + (n + 1) * TILE)
            term = contract(xs_ref[:, part], held_ref[part, to], ((1,), (0,)))
            both.append(sum_ref[:, to] + term)
        gate, up = both
        act = (gate / (1.0 + jnp.exp(-gate)) * up).astype(bf16)
        at = n * STRIDE
        o_ref[:, :, at : at + TILE] = act[: 2 * EXPERTS].reshape(EXPERTS, 2, TILE)
        o_ref[:, :, at + TILE : at + STRIDE] = act[2 * EXPERTS :].reshape(EXPERTS, 2, TILE // 2)


def expert(x, w):
    rows = 3 * EXPERTS
    x = pltpu.with_memory_space_constraint(x, pltpu.VMEM)
    return pl.pallas_call(
        expert_kernel,
        out_shape=pltpu.HBM((EXPERTS, 2, TILES * STRIDE), bf16),
        in_specs=[vmem(), pl.BlockSpec(memory_space=pltpu.HBM)],
        out_specs=pl.BlockSpec((EXPERTS, 2, TILES * STRIDE), lambda: (0, 0, 0)),
        scratch_shapes=[
            pltpu.VMEM((rows, D), bf16),
            pltpu.VMEM((D, 2 * EH), bf16),
            pltpu.VMEM((rows, 2 * EH), f32),
            pltpu.SemaphoreType.DMA((PIECES,)),
        ],
        compiler_params=params(40),
        cost_estimate=cost(2 * rows * D * 2 * EH, 18 * MIB, rows * EH),
        name="expert_rows",
    )(x, in_hbm(w))


def unpack_kernel(ids_ref, weight_ref, back_ref, o_ref):
    ids = ids_ref[...]
    mask_a, mask_b = slot_masks(ids)
    slot_a = lax.shift_right_logical(
        lax.broadcasted_iota(jnp.int32, (2 * EXPERTS, ROWS), 0), 1
    )
    slot_b = lax.broadcasted_iota(jnp.int32, (EXPERTS, ROWS), 0)
    pick_a = [jnp.where(ids[c : c + 1, :] == slot_a, mask_a, 0.0) for c in range(TOPK)]
    pick_b = [jnp.where(ids[c : c + 1, :] == slot_b, mask_b, 0.0) for c in range(TOPK)]
    pick_a = jnp.concatenate(pick_a, axis=1).astype(bf16)
    pick_b = jnp.concatenate(pick_b, axis=1).astype(bf16)
    for n in range(TILES):
        at = n * STRIDE
        slots = back_ref[:, :, at : at + TILE].reshape(2 * EXPERTS, TILE)
        third = back_ref[:, :, at + TILE : at + STRIDE].reshape(EXPERTS, TILE)
        found = contract(pick_a, slots, ((0,), (0,))) + contract(pick_b, third, ((0,), (0,)))
        for c in range(TOPK):
            to = c * EH + n * TILE
            part = weight_ref[:, c : c + 1] * found[c * ROWS : (c + 1) * ROWS]
            o_ref[:, to : to + TILE] = part.astype(bf16)


def unpack(ids, weights, back):
    return pl.pallas_call(
        unpack_kernel,
        out_shape=jax.ShapeDtypeStruct((ROWS, TOPK * EH), bf16),
        in_specs=[vmem()] * 3,
        out_specs=vmem(),
        compiler_params=params(16),
        cost_estimate=cost(2 * 384 * EXPERTS * EH, 2 * MIB),
        name="unpack_rows",
    )(ids, weights, back)


def query_kernel(rep_ref, nope_ref, comp_ref, from_same_ref, from_cross_ref, other_ref, rise_q_ref,
                 rise_k_ref, down_k_ref, down_q_ref, base_ref, own_ref, same_ref, cross_ref,
                 guest_ref, low_ref, rq_ref, rk_ref, dk_ref, dq_ref):
    step = pl.program_id(0)

    @pl.when(step == 0)
    def _():
        @pl.when(rep_ref[0] == 0)
        def _():
            rq_ref[...] = rise_q_ref[...]
            rk_ref[...] = rise_k_ref[...]
            dk_ref[...] = down_k_ref[...]
            dq_ref[...] = down_q_ref[...]

        @pl.when(rep_ref[0] != 0)
        def _():
            for ref, at, width in (
                (rq_ref, RISE_Q_AT, HCOLS),
                (rk_ref, RISE_K_AT, HCOLS),
                (dk_ref, DOWN_K_AT, LATENT),
                (dq_ref, DOWN_Q_AT, QLORA),
            ):
                ref[:QUARTER] = from_same_ref[:, at : at + width]
                ref[QUARTER : 2 * QUARTER] = from_cross_ref[:, at : at + width]
                at -= RISE_Q_AT
                ref[2 * QUARTER :] = other_ref[:, at : at + width]

        guest_ref[:, :PATH_COLS] = from_same_ref[:, :PATH_COLS]
        guest_ref[:, PATH_COLS:] = from_cross_ref[:, :PATH_COLS]
        down = dq_ref[...]
        comp = (
            comp_ref[...],
            from_same_ref[:, COMP_AT : COMP_AT + QLORA],
            from_cross_ref[:, COMP_AT : COMP_AT + QLORA],
        )
        for k in range(3):
            low = contract(comp[k], down, ((1,), (1,)))
            low_ref[k * ROWS : (k + 1) * ROWS] = low.astype(bf16)

    cols = pl.ds(pl.multiple_of(step * GROUP * NOPE, GROUP * NOPE), GROUP * NOPE)
    path = lax.div(step, 2)
    guest = pl.ds(pl.multiple_of((1 + path) * ROWS, ROWS), ROWS)
    low = jnp.concatenate([low_ref[:ROWS], low_ref[guest]], axis=0)
    nope = jnp.concatenate([nope_ref[...], guest_ref[:, cols]], axis=0)
    delta = contract(low, rq_ref[:, cols], ((1,), (0,)))
    heads = (nope.astype(f32) + delta).astype(bf16)
    rise = rk_ref[:, cols]
    down = dk_ref[...]
    kept = []
    for h in range(GROUP):
        query = heads[:, h * NOPE : (h + 1) * NOPE]
        mixed = contract(query, rise[:, h * NOPE : (h + 1) * NOPE], ((1,), (1,)))
        high = mixed.astype(bf16)
        rest = (mixed - high.astype(f32)).astype(bf16)
        latent = (
            contract(query, base_ref[h], ((1,), (0,)))
            + contract(high, down, ((1,), (0,)))
            + contract(rest, down, ((1,), (0,)))
        )
        own_ref[h] = latent[:ROWS].astype(bf16)
        kept.append(latent[ROWS:].astype(bf16))

    @pl.when(path == 0)
    def _():
        for h in range(GROUP):
            same_ref[h] = kept[h]

    @pl.when(path != 0)
    def _():
        for h in range(GROUP):
            cross_ref[h] = kept[h]


def query_part(rep, nope, comp, from_same, from_cross, other, rise_q, rise_k, down_k, down_q, base):
    steps = HALF // GROUP
    block = (GROUP, ROWS, LATENT)
    return pl.pallas_call(
        query_kernel,
        out_shape=(
            jax.ShapeDtypeStruct((HALF, ROWS, LATENT), bf16),
            jax.ShapeDtypeStruct((HALF // 2, ROWS, LATENT), bf16),
            jax.ShapeDtypeStruct((HALF // 2, ROWS, LATENT), bf16),
        ),
        grid_spec=pltpu.PrefetchScalarGridSpec(
            num_scalar_prefetch=1,
            grid=(steps,),
            in_specs=[
                pl.BlockSpec((ROWS, GROUP * NOPE), lambda g, r: (0, r[0] * steps + g)),
                pl.BlockSpec((ROWS, QLORA), lambda g, r: (0, 0)),
                pl.BlockSpec((ROWS, PAYLOAD), lambda g, r: (0, 0)),
                pl.BlockSpec((ROWS, PAYLOAD), lambda g, r: (0, 0)),
                pl.BlockSpec((2 * QUARTER, PAYLOAD - RISE_Q_AT), lambda g, r: (0, 0)),
                pl.BlockSpec((RANK, HCOLS), lambda g, r: (0, 0)),
                pl.BlockSpec((RANK, HCOLS), lambda g, r: (0, 0)),
                pl.BlockSpec((RANK, LATENT), lambda g, r: (0, 0)),
                pl.BlockSpec((RANK, QLORA), lambda g, r: (0, 0)),
                pl.BlockSpec((GROUP, NOPE, LATENT), lambda g, r: (g, 0, 0)),
            ],
            out_specs=(
                pl.BlockSpec(block, lambda g, r: (g, 0, 0)),
                pl.BlockSpec(block, lambda g, r: (jnp.minimum(g, 1), 0, 0)),
                pl.BlockSpec(block, lambda g, r: (jnp.maximum(g - 2, 0), 0, 0)),
            ),
            scratch_shapes=[
                pltpu.VMEM((ROWS, HCOLS), bf16),
                pltpu.VMEM((3 * ROWS, RANK), bf16),
                pltpu.VMEM((RANK, HCOLS), bf16),
                pltpu.VMEM((RANK, HCOLS), bf16),
                pltpu.VMEM((RANK, LATENT), bf16),
                pltpu.VMEM((RANK, QLORA), bf16),
            ],
        ),
        compiler_params=params(24),
        cost_estimate=cost(20000000000, 1 << 10),
        name="query_latent",
    )(rep, in_hbm(nope), comp, from_same, from_cross, other, *map(in_hbm, (rise_q, rise_k, down_k, down_q, base)))


BATCH = 2
LANES = LATENT // 128


def attend_kernel(lengths_ref, rep_ref, own_ref, same_ref, cross_ref, rope_ref, kv_ref,
                  o_ref, query_ref, done_ref):
    step = pl.program_id(0)

    @pl.when(step == 0)
    def _():
        mine = rep_ref[0] * HALF
        other = HALF - mine
        for h in range(HALF):
            at = pl.multiple_of((mine + h) * ROWS, ROWS)
            value = own_ref[h].astype(f32)
            for j in range(LANES):
                query_ref[j, pl.ds(at, ROWS), :] = value[:, j * 128 : (j + 1) * 128]
        for k, ref in enumerate((same_ref, cross_ref)):
            for h in range(HALF // 2):
                at = pl.multiple_of((other + k * (HALF // 2) + h) * ROWS, ROWS)
                value = ref[h].astype(f32)
                for j in range(LANES):
                    query_ref[j, pl.ds(at, ROWS), :] = value[:, j * 128 : (j + 1) * 128]

    for b in range(BATCH):
        row = step * BATCH + b
        query = jnp.concatenate(
            [query_ref[j, pl.ds(row, HEADS, stride=ROWS), :] for j in range(LANES)], axis=1
        ).astype(bf16)
        kv = kv_ref[b]
        scores = contract(query, kv[:, :LATENT], ((1,), (1,))) + contract(
            rope_ref[b], kv[:, LATENT:], ((1,), (1,))
        )
        scores = scores * (1.0 / (NOPE + ROPE) ** 0.5)
        live = lax.broadcasted_iota(jnp.int32, scores.shape, 1) < lengths_ref[row]
        scores = jnp.where(live, scores, -1e30)
        highest = jnp.max(scores, axis=1, keepdims=True)
        exponent = jnp.where(live, jnp.exp(scores - highest), 0.0)
        weights = (exponent / jnp.sum(exponent, axis=1, keepdims=True)).astype(bf16)
        at = pl.multiple_of(row * HEADS, HEADS)
        latent = contract(weights, kv[:, :LATENT], ((1,), (0,)))
        for j in range(LANES):
            done_ref[j, pl.ds(at, HEADS), :] = latent[:, j * 128 : (j + 1) * 128]

    @pl.when(step == pl.num_programs(0) - 1)
    def _():
        for h in range(HEADS):
            for j in range(LANES):
                at = h * LATENT + j * 128
                o_ref[:, at : at + 128] = done_ref[
                    j, pl.ds(h, ROWS, stride=HEADS), :
                ].astype(bf16)


def attend(lengths, rep, own, same, cross, rope, kv):
    whole = lambda s, *_: (0, 0, 0)
    half = pl.BlockSpec((HALF // 2, ROWS, LATENT), whole)
    return pl.pallas_call(
        attend_kernel,
        out_shape=jax.ShapeDtypeStruct((ROWS, HEADS * LATENT), bf16),
        grid_spec=pltpu.PrefetchScalarGridSpec(
            num_scalar_prefetch=2,
            grid=(ROWS // BATCH,),
            in_specs=[
                pl.BlockSpec((HALF, ROWS, LATENT), whole),
                half,
                half,
                pl.BlockSpec((BATCH, HEADS, ROPE), lambda s, *_: (s, 0, 0)),
                pl.BlockSpec((BATCH, LEN, LATENT + ROPE), lambda s, *_: (s, 0, 0)),
            ],
            out_specs=pl.BlockSpec((ROWS, HEADS * LATENT), lambda s, *_: (0, 0)),
            scratch_shapes=[
                pltpu.VMEM((LANES, HEADS * ROWS, 128), f32),
                pltpu.VMEM((LANES, ROWS * HEADS, 128), f32),
            ],
        ),
        compiler_params=params(40),
        cost_estimate=cost(2 * ROWS * HEADS * LEN * 1088, 6 * MIB, ROWS * HEADS * LEN),
        name="attend_rows",
    )(lengths, rep, own, same, cross, rope, in_hbm(kv))


def on_device(
    query_nope,
    query_rope,
    query_compressed,
    kv_cache,
    cache_lengths,
    key_base,
    query_down,
    query_rise,
    key_down,
    key_rise,
    moe_input,
    expert_ids,
    route_weights,
    expert_gate_up,
):
    rep = lax.axis_index("rep")
    core = lax.axis_index("ep") % 2
    ep_size = lax.axis_size("ep")
    every = [(r, e) for r in range(2) for e in range(ep_size)]
    place = lambda r, e: r * ep_size + e
    to_same = [(place(r, e), place(1 - r, e)) for r, e in every]
    to_cross = [(place(r, e), place(1 - r, e ^ 2)) for r, e in every]
    to_core = [(e, e ^ 1) for e in range(ep_size)]

    factors = (query_rise[0], key_rise[0], key_down[0], query_down[0].T)
    same, cross = payloads(jnp.stack([rep, core]), query_nope, query_compressed, *factors)
    moe_input, same, cross = lax.optimization_barrier((moe_input, same, cross))
    leaving_rows = pack(expert_ids.T, moe_input)
    arrived_rows = lax.all_to_all(leaving_rows, AXES, 0, 0, tiled=True)

    from_same = lax.ppermute(same, AXES, to_same)
    from_cross = lax.ppermute(cross, AXES, to_cross)
    half = jnp.concatenate([from_same[:, RISE_Q_AT:], from_cross[:, RISE_Q_AT:]], axis=0)
    other = lax.ppermute(half, "ep", to_core)
    own, same, cross = query_part(
        rep.reshape(1), query_nope, query_compressed, from_same, from_cross, other, *factors, key_base
    )
    same = lax.ppermute(same, AXES, to_same)
    cross = lax.ppermute(cross, AXES, to_cross)
    arrived_rows, own = lax.optimization_barrier((arrived_rows, own))
    rope = query_rope.reshape(ROWS, HEADS, ROPE)
    activation = expert(arrived_rows, expert_gate_up)
    activation, same, cross = lax.optimization_barrier((activation, same, cross))
    back = lax.all_to_all(activation, AXES, 0, 0, tiled=True)
    attended = attend(cache_lengths, rep.reshape(1), own, same, cross, rope, kv_cache)
    expert_hidden = unpack(expert_ids.T, route_weights, back)
    return (attended, expert_hidden)


def solution(mesh):
    both = ("rep", "ep")
    return jax.shard_map(
        on_device,
        mesh=mesh,
        in_specs=(
            P(both, None),
            P(both, None),
            P(both, None),
            P(both, None, None),
            P(both),
            P("rep", None, None),
            P("rep", None, None),
            P("rep", None, None),
            P("rep", None, None),
            P("rep", None, None),
            P(both, None),
            P(both, None),
            P(both, None),
            P(both, None, None),
        ),
        out_specs=(P(both, None), P(both, None)),
        check_vma=False,
    )
```

```python
import functools

import jax
import jax.numpy as jnp
from jax import lax
from jax.experimental import pallas as pl
from jax.experimental.pallas import tpu as pltpu
from jax.sharding import PartitionSpec as P

HEADS = 64
NOPE = 128
ROPE = 64
LATENT = 512
RANK = 64
QLORA = 1536
D = 3584
EH = 1024
TOPK = 8
ROWS = 16
LEN = 192
EXPERTS = 128
HALF = HEADS // 2
HCOLS = HALF * NOPE
GROUP = 8
PATH_COLS = HCOLS // 2
QUARTER = RANK // 4
COMP_AT = PATH_COLS
RISE_Q_AT = COMP_AT + QLORA
RISE_K_AT = RISE_Q_AT + HCOLS
DOWN_K_AT = RISE_K_AT + HCOLS
DOWN_Q_AT = DOWN_K_AT + LATENT
PAYLOAD = DOWN_Q_AT + QLORA
AXES = ("rep", "ep")
MIB = 1 << 20

f32 = jnp.float32
bf16 = jnp.bfloat16


def contract(a, b, dims):
    return lax.dot_general(a, b, (dims, ((), ())), preferred_element_type=f32)


def vmem():
    return pl.BlockSpec(memory_space=pltpu.VMEM)


def in_hbm(x):
    return pltpu.with_memory_space_constraint(x, pltpu.HBM)


def params(mib, **more):
    return pltpu.CompilerParams(vmem_limit_bytes=mib * MIB, **more)


def cost(flops, moved, exps=0):
    return pl.CostEstimate(flops=flops, bytes_accessed=moved, transcendentals=exps)


def named_and_rank(ids, slots, shift):
    expert = lax.broadcasted_iota(jnp.int32, (slots, ROWS), 0)
    if shift:
        expert = lax.shift_right_logical(expert, shift)
    named = jnp.zeros((slots, ROWS), f32)
    for c in range(TOPK):
        named = jnp.where(ids[c : c + 1, :] == expert, 1.0, named)
    above = lax.broadcasted_iota(jnp.int32, (ROWS, ROWS), 0) < lax.broadcasted_iota(
        jnp.int32, (ROWS, ROWS), 1
    )
    rank = contract(named.astype(bf16), above.astype(bf16), ((1,), (0,)))
    return named, rank


def slot_masks(ids):
    named, rank = named_and_rank(ids, 2 * EXPERTS, 1)
    slot = lax.broadcasted_iota(jnp.int32, (2 * EXPERTS, ROWS), 0) & 1
    mask_a = jnp.where(rank == slot.astype(f32), named, 0.0)
    named, rank = named_and_rank(ids, EXPERTS, 0)
    mask_b = jnp.where(rank == 2.0, named, 0.0)
    return mask_a, mask_b


PIECE = 512
PIECES = D // PIECE
TAKEN = (1, 1, 2, 2, 1)
SPAN = PIECE + PIECE // 2
TILE = 256
TILES = EH // TILE
STRIDE = TILE + TILE // 2


def leave_kernel(place_ref, ids_ref, x_ref, nope_ref, comp_ref, rise_q_ref, rise_k_ref, down_k_ref,
                 down_q_ref, o_ref, same_ref, cross_ref, packed_ref, sent, queued):
    rep, core = place_ref[0], place_ref[1]
    gathered = []
    for path in range(2):
        at = pl.multiple_of((1 - rep) * HCOLS + path * PATH_COLS, 128)
        rows = pl.ds(pl.multiple_of((core * 2 + path) * QUARTER, QUARTER), QUARTER)
        for source, to, width in (
            (nope_ref.at[:, pl.ds(at, PATH_COLS)], 0, PATH_COLS),
            (comp_ref, COMP_AT, QLORA),
            (rise_q_ref.at[rows, pl.ds(HCOLS, HCOLS)], RISE_Q_AT, HCOLS),
            (rise_k_ref.at[rows, pl.ds(HCOLS, HCOLS)], RISE_K_AT, HCOLS),
            (down_k_ref.at[rows, :], DOWN_K_AT, LATENT),
            (down_q_ref.at[rows, :], DOWN_Q_AT, QLORA),
        ):
            copy = pltpu.make_async_copy(
                source,
                (same_ref, cross_ref)[path].at[:, pl.ds(to, width)],
                queued.at[len(gathered)],
            )
            copy.start()
            gathered.append(copy)

    mask_a, mask_b = slot_masks(ids_ref[...])
    mask_a, mask_b = mask_a.astype(bf16), mask_b.astype(bf16)
    copies = []
    for g in range(PIECES):
        x = x_ref[:, g * PIECE : (g + 1) * PIECE]
        at = g * SPAN
        rows = contract(mask_a, x, ((1,), (0,))).astype(bf16)
        packed_ref[:, :, at : at + PIECE] = rows.reshape(EXPERTS, 2, PIECE)
        rows = contract(mask_b, x, ((1,), (0,))).astype(bf16)
        packed_ref[:, :, at + PIECE : at + SPAN] = rows.reshape(EXPERTS, 2, PIECE // 2)
        lanes = pl.ds(at, SPAN)
        copy = pltpu.make_async_copy(
            packed_ref.at[:, :, lanes], o_ref.at[:, :, lanes], sent.at[g]
        )
        copy.start()
        copies.append(copy)
    for copy in gathered + copies:
        copy.wait()


def leave(place, ids, x, nope, comp, rise_q, rise_k, down_k, down_q):
    shape = (EXPERTS, 2, PIECES * SPAN)
    hbm = pl.BlockSpec(memory_space=pltpu.HBM)
    return pl.pallas_call(
        leave_kernel,
        out_shape=(
            pltpu.HBM(shape, bf16),
            pltpu.VMEM((ROWS, PAYLOAD), bf16),
            pltpu.VMEM((ROWS, PAYLOAD), bf16),
        ),
        in_specs=[pl.BlockSpec(memory_space=pltpu.SMEM), vmem(), vmem()] + [hbm] * 6,
        out_specs=(hbm, vmem(), vmem()),
        scratch_shapes=[
            pltpu.VMEM(shape, bf16),
            pltpu.SemaphoreType.DMA((PIECES,)),
            pltpu.SemaphoreType.DMA((12,)),
        ],
        compiler_params=params(16),
        cost_estimate=cost(2 * 384 * ROWS * D, 3 * MIB),
        name="leave",
    )(place, in_hbm(ids), in_hbm(x), *map(in_hbm, (nope, comp, rise_q, rise_k, down_k, down_q)))


def expert_kernel(x_ref, w_ref, o_ref, xs_ref, held_ref, sum_ref, act_ref, came, left):
    rows, wide = 3 * EXPERTS, 2 * TILE
    copies, leaving = [], []
    for g in range(PIECES):
        part = pl.ds(g * PIECE, PIECE)
        copy = pltpu.make_async_copy(w_ref.at[0, part, :], held_ref.at[part, :], came.at[g])
        copy.start()
        copies.append(copy)
    for g in range(PIECES):
        at, to = g * SPAN, slice(g * PIECE, (g + 1) * PIECE)
        xs_ref[: 2 * EXPERTS, to] = x_ref[:, :, at : at + PIECE].reshape(2 * EXPERTS, PIECE)
        xs_ref[2 * EXPERTS :, to] = x_ref[:, :, at + PIECE : at + SPAN].reshape(EXPERTS, PIECE)
    done = 0
    for take in TAKEN[:-1]:
        for g in range(done, done + take):
            copies[g].wait()
        part = slice(done * PIECE, (done + take) * PIECE)
        for n in range(2 * EH // wide):
            to = slice(n * wide, (n + 1) * wide)
            term = contract(xs_ref[:, part], held_ref[part, to], ((1,), (0,)))
            sum_ref[:, to] = term if done == 0 else sum_ref[:, to] + term
        done += take
    for g in range(done, PIECES):
        copies[g].wait()
    part = slice(done * PIECE, D)
    for n in range(TILES):
        both = []
        for k in range(2):
            to = slice(k * EH + n * TILE, k * EH + (n + 1) * TILE)
            term = contract(xs_ref[:, part], held_ref[part, to], ((1,), (0,)))
            both.append(sum_ref[:, to] + term)
        gate, up = both
        act = (gate / (1.0 + jnp.exp(-gate)) * up).astype(bf16)
        at = n * STRIDE
        act_ref[:, :, at : at + TILE] = act[: 2 * EXPERTS].reshape(EXPERTS, 2, TILE)
        act_ref[:, :, at + TILE : at + STRIDE] = act[2 * EXPERTS :].reshape(EXPERTS, 2, TILE // 2)
        lanes = pl.ds(at, STRIDE)
        copy = pltpu.make_async_copy(act_ref.at[:, :, lanes], o_ref.at[:, :, lanes], left.at[n])
        copy.start()
        leaving.append(copy)
    for copy in leaving:
        copy.wait()


def expert(x, w):
    rows = 3 * EXPERTS
    x = pltpu.with_memory_space_constraint(x, pltpu.VMEM)
    return pl.pallas_call(
        expert_kernel,
        out_shape=pltpu.HBM((EXPERTS, 2, TILES * STRIDE), bf16),
        in_specs=[vmem(), pl.BlockSpec(memory_space=pltpu.HBM)],
        out_specs=pl.BlockSpec(memory_space=pltpu.HBM),
        scratch_shapes=[
            pltpu.VMEM((rows, D), bf16),
            pltpu.VMEM((D, 2 * EH), bf16),
            pltpu.VMEM((rows, 2 * EH), f32),
            pltpu.VMEM((EXPERTS, 2, TILES * STRIDE), bf16),
            pltpu.SemaphoreType.DMA((PIECES,)),
            pltpu.SemaphoreType.DMA((TILES,)),
        ],
        compiler_params=params(40),
        cost_estimate=cost(2 * rows * D * 2 * EH, 18 * MIB, rows * EH),
        name="expert_rows",
    )(x, in_hbm(w))


def picks_kernel(ids_ref, a_ref, b_ref):
    ids = ids_ref[...]
    mask_a, mask_b = slot_masks(ids)
    slot_a = lax.shift_right_logical(
        lax.broadcasted_iota(jnp.int32, (2 * EXPERTS, ROWS), 0), 1
    )
    slot_b = lax.broadcasted_iota(jnp.int32, (EXPERTS, ROWS), 0)
    pick_a = [jnp.where(ids[c : c + 1, :] == slot_a, mask_a, 0.0) for c in range(TOPK)]
    pick_b = [jnp.where(ids[c : c + 1, :] == slot_b, mask_b, 0.0) for c in range(TOPK)]
    a_ref[...] = jnp.concatenate(pick_a, axis=1).T.astype(bf16)
    b_ref[...] = jnp.concatenate(pick_b, axis=1).T.astype(bf16)


def picks(ids):
    entries = TOPK * ROWS
    return pl.pallas_call(
        picks_kernel,
        out_shape=(
            jax.ShapeDtypeStruct((entries, 2 * EXPERTS), bf16),
            jax.ShapeDtypeStruct((entries, EXPERTS), bf16),
        ),
        in_specs=[vmem()],
        out_specs=(vmem(), vmem()),
        compiler_params=params(16),
        cost_estimate=cost(1 << 10, 1 << 10),
        name="picks",
    )(ids)


def unpack_kernel(pick_a_ref, pick_b_ref, weight_ref, back_ref, o_ref):
    for n in range(TILES):
        at = n * STRIDE
        slots = back_ref[:, :, at : at + TILE].reshape(2 * EXPERTS, TILE)
        third = back_ref[:, :, at + TILE : at + STRIDE].reshape(EXPERTS, TILE)
        found = contract(pick_a_ref[...], slots, ((1,), (0,))) + contract(
            pick_b_ref[...], third, ((1,), (0,))
        )
        for c in range(TOPK):
            to = c * EH + n * TILE
            part = weight_ref[:, c : c + 1] * found[c * ROWS : (c + 1) * ROWS]
            o_ref[:, to : to + TILE] = part.astype(bf16)


def unpack(pick_a, pick_b, weights, back):
    return pl.pallas_call(
        unpack_kernel,
        out_shape=jax.ShapeDtypeStruct((ROWS, TOPK * EH), bf16),
        in_specs=[vmem()] * 4,
        out_specs=vmem(),
        compiler_params=params(16),
        cost_estimate=cost(2 * 384 * EXPERTS * EH, 2 * MIB),
        name="unpack_rows",
    )(pick_a, pick_b, weights, back)


def query_kernel(rep_ref, nope_ref, comp_ref, from_same_ref, from_cross_ref, other_ref, rise_q_ref,
                 rise_k_ref, down_k_ref, down_q_ref, base_ref, own_ref, same_ref, cross_ref,
                 guest_ref, low_ref, rq_ref, rk_ref, dk_ref, dq_ref):
    step = pl.program_id(0)

    @pl.when(step == 0)
    def _():
        @pl.when(rep_ref[0] == 0)
        def _():
            rq_ref[...] = rise_q_ref[...]
            rk_ref[...] = rise_k_ref[...]
            dk_ref[...] = down_k_ref[...]
            dq_ref[...] = down_q_ref[...]

        @pl.when(rep_ref[0] != 0)
        def _():
            for ref, at, width in (
                (rq_ref, RISE_Q_AT, HCOLS),
                (rk_ref, RISE_K_AT, HCOLS),
                (dk_ref, DOWN_K_AT, LATENT),
                (dq_ref, DOWN_Q_AT, QLORA),
            ):
                ref[:QUARTER] = from_same_ref[:, at : at + width]
                ref[QUARTER : 2 * QUARTER] = from_cross_ref[:, at : at + width]
                at -= RISE_Q_AT
                ref[2 * QUARTER :] = other_ref[:, at : at + width]

        guest_ref[:, :PATH_COLS] = from_same_ref[:, :PATH_COLS]
        guest_ref[:, PATH_COLS:] = from_cross_ref[:, :PATH_COLS]
        down = dq_ref[...]
        comp = (
            comp_ref[...],
            from_same_ref[:, COMP_AT : COMP_AT + QLORA],
            from_cross_ref[:, COMP_AT : COMP_AT + QLORA],
        )
        for k in range(3):
            low = contract(comp[k], down, ((1,), (1,)))
            low_ref[k * ROWS : (k + 1) * ROWS] = low.astype(bf16)

    cols = pl.ds(pl.multiple_of(step * GROUP * NOPE, GROUP * NOPE), GROUP * NOPE)
    path = lax.div(step, 2)
    guest = pl.ds(pl.multiple_of((1 + path) * ROWS, ROWS), ROWS)
    low = jnp.concatenate([low_ref[:ROWS], low_ref[guest]], axis=0)
    nope = jnp.concatenate([nope_ref[...], guest_ref[:, cols]], axis=0)
    delta = contract(low, rq_ref[:, cols], ((1,), (0,)))
    heads = (nope.astype(f32) + delta).astype(bf16)
    rise = rk_ref[:, cols]
    down = dk_ref[...]
    kept = []
    for h in range(GROUP):
        query = heads[:, h * NOPE : (h + 1) * NOPE]
        mixed = contract(query, rise[:, h * NOPE : (h + 1) * NOPE], ((1,), (1,)))
        high = mixed.astype(bf16)
        rest = (mixed - high.astype(f32)).astype(bf16)
        latent = (
            contract(query, base_ref[h], ((1,), (0,)))
            + contract(high, down, ((1,), (0,)))
            + contract(rest, down, ((1,), (0,)))
        )
        own_ref[h] = latent[:ROWS].astype(bf16)
        kept.append(latent[ROWS:].astype(bf16))

    @pl.when(path == 0)
    def _():
        for h in range(GROUP):
            same_ref[h] = kept[h]

    @pl.when(path != 0)
    def _():
        for h in range(GROUP):
            cross_ref[h] = kept[h]


def query_part(rep, nope, comp, from_same, from_cross, other, rise_q, rise_k, down_k, down_q, base):
    steps = HALF // GROUP
    block = (GROUP, ROWS, LATENT)
    return pl.pallas_call(
        query_kernel,
        out_shape=(
            jax.ShapeDtypeStruct((HALF, ROWS, LATENT), bf16),
            jax.ShapeDtypeStruct((HALF // 2, ROWS, LATENT), bf16),
            jax.ShapeDtypeStruct((HALF // 2, ROWS, LATENT), bf16),
        ),
        grid_spec=pltpu.PrefetchScalarGridSpec(
            num_scalar_prefetch=1,
            grid=(steps,),
            in_specs=[
                pl.BlockSpec((ROWS, GROUP * NOPE), lambda g, r: (0, r[0] * steps + g)),
                pl.BlockSpec((ROWS, QLORA), lambda g, r: (0, 0)),
                pl.BlockSpec((ROWS, PAYLOAD), lambda g, r: (0, 0)),
                pl.BlockSpec((ROWS, PAYLOAD), lambda g, r: (0, 0)),
                pl.BlockSpec((2 * QUARTER, PAYLOAD - RISE_Q_AT), lambda g, r: (0, 0)),
                pl.BlockSpec((RANK, HCOLS), lambda g, r: (0, 0)),
                pl.BlockSpec((RANK, HCOLS), lambda g, r: (0, 0)),
                pl.BlockSpec((RANK, LATENT), lambda g, r: (0, 0)),
                pl.BlockSpec((RANK, QLORA), lambda g, r: (0, 0)),
                pl.BlockSpec((GROUP, NOPE, LATENT), lambda g, r: (g, 0, 0)),
            ],
            out_specs=(
                pl.BlockSpec(block, lambda g, r: (g, 0, 0)),
                pl.BlockSpec(block, lambda g, r: (jnp.minimum(g, 1), 0, 0)),
                pl.BlockSpec(block, lambda g, r: (jnp.maximum(g - 2, 0), 0, 0)),
            ),
            scratch_shapes=[
                pltpu.VMEM((ROWS, HCOLS), bf16),
                pltpu.VMEM((3 * ROWS, RANK), bf16),
                pltpu.VMEM((RANK, HCOLS), bf16),
                pltpu.VMEM((RANK, HCOLS), bf16),
                pltpu.VMEM((RANK, LATENT), bf16),
                pltpu.VMEM((RANK, QLORA), bf16),
            ],
        ),
        compiler_params=params(24),
        cost_estimate=cost(20000000000, 1 << 10),
        name="query_latent",
    )(rep, in_hbm(nope), comp, from_same, from_cross, other, *map(in_hbm, (rise_q, rise_k, down_k, down_q, base)))


BATCH = 2
LANES = LATENT // 128


def attend_kernel(lengths_ref, rep_ref, own_ref, same_ref, cross_ref, rope_ref, kv_ref,
                  o_ref, query_ref, done_ref):
    step = pl.program_id(0)

    @pl.when(step == 0)
    def _():
        mine = rep_ref[0] * HALF
        other = HALF - mine
        for h in range(HALF):
            at = pl.multiple_of((mine + h) * ROWS, ROWS)
            value = own_ref[h].astype(f32)
            for j in range(LANES):
                query_ref[j, pl.ds(at, ROWS), :] = value[:, j * 128 : (j + 1) * 128]
        for k, ref in enumerate((same_ref, cross_ref)):
            for h in range(HALF // 2):
                at = pl.multiple_of((other + k * (HALF // 2) + h) * ROWS, ROWS)
                value = ref[h].astype(f32)
                for j in range(LANES):
                    query_ref[j, pl.ds(at, ROWS), :] = value[:, j * 128 : (j + 1) * 128]

    for b in range(BATCH):
        row = step * BATCH + b
        query = jnp.concatenate(
            [query_ref[j, pl.ds(row, HEADS, stride=ROWS), :] for j in range(LANES)], axis=1
        ).astype(bf16)
        kv = kv_ref[b]
        scores = contract(query, kv[:, :LATENT], ((1,), (1,))) + contract(
            rope_ref[b], kv[:, LATENT:], ((1,), (1,))
        )
        scores = scores * (1.0 / (NOPE + ROPE) ** 0.5)
        live = lax.broadcasted_iota(jnp.int32, scores.shape, 1) < lengths_ref[row]
        scores = jnp.where(live, scores, -1e30)
        highest = jnp.max(scores, axis=1, keepdims=True)
        exponent = jnp.where(live, jnp.exp(scores - highest), 0.0)
        weights = (exponent / jnp.sum(exponent, axis=1, keepdims=True)).astype(bf16)
        at = pl.multiple_of(row * HEADS, HEADS)
        latent = contract(weights, kv[:, :LATENT], ((1,), (0,)))
        for j in range(LANES):
            done_ref[j, pl.ds(at, HEADS), :] = latent[:, j * 128 : (j + 1) * 128]

    @pl.when(step == pl.num_programs(0) - 1)
    def _():
        for h in range(HEADS):
            for j in range(LANES):
                at = h * LATENT + j * 128
                o_ref[:, at : at + 128] = done_ref[
                    j, pl.ds(h, ROWS, stride=HEADS), :
                ].astype(bf16)


def attend(lengths, rep, own, same, cross, rope, kv):
    whole = lambda s, *_: (0, 0, 0)
    half = pl.BlockSpec((HALF // 2, ROWS, LATENT), whole)
    return pl.pallas_call(
        attend_kernel,
        out_shape=jax.ShapeDtypeStruct((ROWS, HEADS * LATENT), bf16),
        grid_spec=pltpu.PrefetchScalarGridSpec(
            num_scalar_prefetch=2,
            grid=(ROWS // BATCH,),
            in_specs=[
                pl.BlockSpec((HALF, ROWS, LATENT), whole),
                half,
                half,
                pl.BlockSpec((BATCH, HEADS, ROPE), lambda s, *_: (s, 0, 0)),
                pl.BlockSpec((BATCH, LEN, LATENT + ROPE), lambda s, *_: (s, 0, 0)),
            ],
            out_specs=pl.BlockSpec((ROWS, HEADS * LATENT), lambda s, *_: (0, 0)),
            scratch_shapes=[
                pltpu.VMEM((LANES, HEADS * ROWS, 128), f32),
                pltpu.VMEM((LANES, ROWS * HEADS, 128), f32),
            ],
        ),
        compiler_params=params(40),
        cost_estimate=cost(2 * ROWS * HEADS * LEN * 1088, 6 * MIB, ROWS * HEADS * LEN),
        name="attend_rows",
    )(lengths, rep, own, same, cross, rope, in_hbm(kv))


def on_device(
    query_nope,
    query_rope,
    query_compressed,
    kv_cache,
    cache_lengths,
    key_base,
    query_down,
    query_rise,
    key_down,
    key_rise,
    moe_input,
    expert_ids,
    route_weights,
    expert_gate_up,
):
    rep = lax.axis_index("rep")
    core = lax.axis_index("ep") % 2
    ep_size = lax.axis_size("ep")
    every = [(r, e) for r in range(2) for e in range(ep_size)]
    place = lambda r, e: r * ep_size + e
    to_same = [(place(r, e), place(1 - r, e)) for r, e in every]
    to_cross = [(place(r, e), place(1 - r, e ^ 2)) for r, e in every]
    to_core = [(e, e ^ 1) for e in range(ep_size)]

    factors = (query_rise[0], key_rise[0], key_down[0], query_down[0].T)
    ids = expert_ids.T
    leaving_rows, same, cross = leave(
        jnp.stack([rep, core]), ids, moe_input, query_nope, query_compressed, *factors
    )
    arrived_rows = lax.all_to_all(leaving_rows, AXES, 0, 0, tiled=True)

    from_same = lax.ppermute(same, AXES, to_same)
    from_cross = lax.ppermute(cross, AXES, to_cross)
    half = jnp.concatenate([from_same[:, RISE_Q_AT:], from_cross[:, RISE_Q_AT:]], axis=0)
    other = lax.ppermute(half, "ep", to_core)
    own, same, cross = query_part(
        rep.reshape(1), query_nope, query_compressed, from_same, from_cross, other, *factors, key_base
    )
    same = lax.ppermute(same, AXES, to_same)
    cross = lax.ppermute(cross, AXES, to_cross)
    ids, own = lax.optimization_barrier((ids, own))
    pick_a, pick_b = picks(ids)
    arrived_rows, own, pick_a, pick_b = lax.optimization_barrier(
        (arrived_rows, own, pick_a, pick_b)
    )
    rope = query_rope.reshape(ROWS, HEADS, ROPE)
    activation = expert(arrived_rows, expert_gate_up)
    activation, same, cross = lax.optimization_barrier((activation, same, cross))
    back = lax.all_to_all(activation, AXES, 0, 0, tiled=True)
    attended = attend(cache_lengths, rep.reshape(1), own, same, cross, rope, kv_cache)
    expert_hidden = unpack(pick_a, pick_b, route_weights, back)
    return (attended, expert_hidden)


def solution(mesh):
    both = ("rep", "ep")
    return jax.shard_map(
        on_device,
        mesh=mesh,
        in_specs=(
            P(both, None),
            P(both, None),
            P(both, None),
            P(both, None, None),
            P(both),
            P("rep", None, None),
            P("rep", None, None),
            P("rep", None, None),
            P("rep", None, None),
            P("rep", None, None),
            P(both, None),
            P(both, None),
            P(both, None),
            P(both, None, None),
        ),
        out_specs=(P(both, None), P(both, None)),
        check_vma=False,
    )
```

```python
import functools

import jax
import jax.numpy as jnp
from jax import lax
from jax.experimental import pallas as pl
from jax.experimental.pallas import tpu as pltpu
from jax.sharding import PartitionSpec as P

HEADS = 64
NOPE = 128
ROPE = 64
LATENT = 512
RANK = 64
QLORA = 1536
D = 3584
EH = 1024
TOPK = 8
ROWS = 16
LEN = 192
EXPERTS = 128
HALF = HEADS // 2
HCOLS = HALF * NOPE
GROUP = 8
PATH_COLS = HCOLS // 2
QUARTER = RANK // 4
COMP_AT = PATH_COLS
RISE_Q_AT = COMP_AT + QLORA
RISE_K_AT = RISE_Q_AT + HCOLS
DOWN_K_AT = RISE_K_AT + HCOLS
DOWN_Q_AT = DOWN_K_AT + LATENT
PAYLOAD = DOWN_Q_AT + QLORA
AXES = ("rep", "ep")
MIB = 1 << 20

f32 = jnp.float32
bf16 = jnp.bfloat16


def contract(a, b, dims):
    return lax.dot_general(a, b, (dims, ((), ())), preferred_element_type=f32)


def vmem():
    return pl.BlockSpec(memory_space=pltpu.VMEM)


def in_hbm(x):
    return pltpu.with_memory_space_constraint(x, pltpu.HBM)


def params(mib, **more):
    return pltpu.CompilerParams(vmem_limit_bytes=mib * MIB, **more)


def cost(flops, moved, exps=0):
    return pl.CostEstimate(flops=flops, bytes_accessed=moved, transcendentals=exps)


def named_and_rank(ids, slots, shift):
    expert = lax.broadcasted_iota(jnp.int32, (slots, ROWS), 0)
    if shift:
        expert = lax.shift_right_logical(expert, shift)
    named = jnp.zeros((slots, ROWS), f32)
    for c in range(TOPK):
        named = jnp.where(ids[c : c + 1, :] == expert, 1.0, named)
    above = lax.broadcasted_iota(jnp.int32, (ROWS, ROWS), 0) < lax.broadcasted_iota(
        jnp.int32, (ROWS, ROWS), 1
    )
    rank = contract(named.astype(bf16), above.astype(bf16), ((1,), (0,)))
    return named, rank


def slot_masks(ids):
    named, rank = named_and_rank(ids, 2 * EXPERTS, 1)
    slot = lax.broadcasted_iota(jnp.int32, (2 * EXPERTS, ROWS), 0) & 1
    mask_a = jnp.where(rank == slot.astype(f32), named, 0.0)
    named, rank = named_and_rank(ids, EXPERTS, 0)
    mask_b = jnp.where(rank == 2.0, named, 0.0)
    return mask_a, mask_b


PIECE = 512
PIECES = D // PIECE
TAKEN = (1, 1, 2, 2, 1)
SPAN = PIECE + PIECE // 2
TILE = 256
TILES = EH // TILE
STRIDE = TILE + TILE // 2


def payload_kernel(ids_ref, nope_ref, comp_ref, rise_q_ref, rise_k_ref, down_k_ref, down_q_ref,
                   same_ref, cross_ref, a_ref, b_ref, held_ref, done):
    rep, core = lax.axis_index("rep"), lax.rem(lax.axis_index("ep"), 2)
    named = pltpu.make_async_copy(ids_ref, held_ref, done.at[12])
    named.start()
    copies = []
    for path, target in enumerate((same_ref, cross_ref)):
        at = pl.multiple_of((1 - rep) * HCOLS + path * PATH_COLS, 128)
        rows = pl.ds(pl.multiple_of((core * 2 + path) * QUARTER, QUARTER), QUARTER)
        for source, to, width in (
            (rise_q_ref.at[rows, pl.ds(HCOLS, HCOLS)], RISE_Q_AT, HCOLS),
            (rise_k_ref.at[rows, pl.ds(HCOLS, HCOLS)], RISE_K_AT, HCOLS),
            (nope_ref.at[:, pl.ds(at, PATH_COLS)], 0, PATH_COLS),
            (comp_ref, COMP_AT, QLORA),
            (down_k_ref.at[rows, :], DOWN_K_AT, LATENT),
            (down_q_ref.at[rows, :], DOWN_Q_AT, QLORA),
        ):
            copy = pltpu.make_async_copy(
                source, target.at[:, pl.ds(to, width)], done.at[len(copies)]
            )
            copy.start()
            copies.append(copy)
    named.wait()
    mask_a, mask_b = slot_masks(held_ref[...])
    a_ref[...] = mask_a.astype(bf16)
    b_ref[...] = mask_b.astype(bf16)
    for copy in copies:
        copy.wait()


def payloads(ids, nope, comp, rise_q, rise_k, down_k, down_q):
    hbm = pl.BlockSpec(memory_space=pltpu.HBM)
    return pl.pallas_call(
        payload_kernel,
        out_shape=(
            jax.ShapeDtypeStruct((ROWS, PAYLOAD), bf16),
            jax.ShapeDtypeStruct((ROWS, PAYLOAD), bf16),
            jax.ShapeDtypeStruct((2 * EXPERTS, ROWS), bf16),
            jax.ShapeDtypeStruct((EXPERTS, ROWS), bf16),
        ),
        in_specs=[hbm] * 7,
        out_specs=(vmem(),) * 4,
        scratch_shapes=[pltpu.VMEM((TOPK, ROWS), jnp.int32), pltpu.SemaphoreType.DMA((13,))],
        compiler_params=params(16),
        cost_estimate=cost(1 << 10, 1 << 20),
        name="payloads",
    )(*map(in_hbm, (ids, nope, comp, rise_q, rise_k, down_k, down_q)))


def pack_kernel(a_ref, b_ref, x_ref, o_ref, packed_ref, sent):
    mask_a, mask_b = a_ref[...], b_ref[...]
    copies = []
    for g in range(PIECES):
        x = x_ref[:, g * PIECE : (g + 1) * PIECE]
        at = g * SPAN
        rows = contract(mask_a, x, ((1,), (0,))).astype(bf16)
        packed_ref[:, :, at : at + PIECE] = rows.reshape(EXPERTS, 2, PIECE)
        rows = contract(mask_b, x, ((1,), (0,))).astype(bf16)
        packed_ref[:, :, at + PIECE : at + SPAN] = rows.reshape(EXPERTS, 2, PIECE // 2)
        lanes = pl.ds(at, SPAN)
        copy = pltpu.make_async_copy(
            packed_ref.at[:, :, lanes], o_ref.at[:, :, lanes], sent.at[g]
        )
        copy.start()
        copies.append(copy)
    for copy in copies:
        copy.wait()


def pack(mask_a, mask_b, x):
    shape = (EXPERTS, 2, PIECES * SPAN)
    return pl.pallas_call(
        pack_kernel,
        out_shape=pltpu.HBM(shape, bf16),
        in_specs=[vmem(), vmem(), vmem()],
        out_specs=pl.BlockSpec(memory_space=pltpu.HBM),
        scratch_shapes=[pltpu.VMEM(shape, bf16), pltpu.SemaphoreType.DMA((PIECES,))],
        compiler_params=params(16),
        cost_estimate=cost(2 * 384 * ROWS * D, 3 * MIB),
        name="pack_rows",
    )(mask_a, mask_b, x)


def expert_kernel(x_ref, w_ref, o_ref, xs_ref, held_ref, sum_ref, act_ref, came, left):
    rows, wide = 3 * EXPERTS, 2 * TILE
    copies, leaving = [], []
    for g in range(PIECES):
        part = pl.ds(g * PIECE, PIECE)
        copy = pltpu.make_async_copy(w_ref.at[0, part, :], held_ref.at[part, :], came.at[g])
        copy.start()
        copies.append(copy)
    for g in range(PIECES):
        at, to = g * SPAN, slice(g * PIECE, (g + 1) * PIECE)
        xs_ref[: 2 * EXPERTS, to] = x_ref[:, :, at : at + PIECE].reshape(2 * EXPERTS, PIECE)
        xs_ref[2 * EXPERTS :, to] = x_ref[:, :, at + PIECE : at + SPAN].reshape(EXPERTS, PIECE)
    done = 0
    for take in TAKEN[:-1]:
        for g in range(done, done + take):
            copies[g].wait()
        part = slice(done * PIECE, (done + take) * PIECE)
        for n in range(2 * EH // wide):
            to = slice(n * wide, (n + 1) * wide)
            term = contract(xs_ref[:, part], held_ref[part, to], ((1,), (0,)))
            sum_ref[:, to] = term if done == 0 else sum_ref[:, to] + term
        done += take
    for g in range(done, PIECES):
        copies[g].wait()
    part = slice(done * PIECE, D)
    for n in range(TILES):
        both = []
        for k in range(2):
            to = slice(k * EH + n * TILE, k * EH + (n + 1) * TILE)
            term = contract(xs_ref[:, part], held_ref[part, to], ((1,), (0,)))
            both.append(sum_ref[:, to] + term)
        gate, up = both
        act = (gate / (1.0 + jnp.exp(-gate)) * up).astype(bf16)
        at = n * STRIDE
        act_ref[:, :, at : at + TILE] = act[: 2 * EXPERTS].reshape(EXPERTS, 2, TILE)
        act_ref[:, :, at + TILE : at + STRIDE] = act[2 * EXPERTS :].reshape(EXPERTS, 2, TILE // 2)
        lanes = pl.ds(at, STRIDE)
        copy = pltpu.make_async_copy(act_ref.at[:, :, lanes], o_ref.at[:, :, lanes], left.at[n])
        copy.start()
        leaving.append(copy)
    for copy in leaving:
        copy.wait()


def expert(x, w):
    rows = 3 * EXPERTS
    x = pltpu.with_memory_space_constraint(x, pltpu.VMEM)
    return pl.pallas_call(
        expert_kernel,
        out_shape=pltpu.HBM((EXPERTS, 2, TILES * STRIDE), bf16),
        in_specs=[vmem(), pl.BlockSpec(memory_space=pltpu.HBM)],
        out_specs=pl.BlockSpec(memory_space=pltpu.HBM),
        scratch_shapes=[
            pltpu.VMEM((rows, D), bf16),
            pltpu.VMEM((D, 2 * EH), bf16),
            pltpu.VMEM((rows, 2 * EH), f32),
            pltpu.VMEM((EXPERTS, 2, TILES * STRIDE), bf16),
            pltpu.SemaphoreType.DMA((PIECES,)),
            pltpu.SemaphoreType.DMA((TILES,)),
        ],
        compiler_params=params(40),
        cost_estimate=cost(2 * rows * D * 2 * EH, 18 * MIB, rows * EH),
        name="expert_rows",
    )(x, in_hbm(w))


def picks_kernel(ids_ref, a_ref, b_ref):
    ids = ids_ref[...]
    mask_a, mask_b = slot_masks(ids)
    slot_a = lax.shift_right_logical(
        lax.broadcasted_iota(jnp.int32, (2 * EXPERTS, ROWS), 0), 1
    )
    slot_b = lax.broadcasted_iota(jnp.int32, (EXPERTS, ROWS), 0)
    pick_a = [jnp.where(ids[c : c + 1, :] == slot_a, mask_a, 0.0) for c in range(TOPK)]
    pick_b = [jnp.where(ids[c : c + 1, :] == slot_b, mask_b, 0.0) for c in range(TOPK)]
    a_ref[...] = jnp.concatenate(pick_a, axis=1).T.astype(bf16)
    b_ref[...] = jnp.concatenate(pick_b, axis=1).T.astype(bf16)


def picks(ids):
    entries = TOPK * ROWS
    return pl.pallas_call(
        picks_kernel,
        out_shape=(
            jax.ShapeDtypeStruct((entries, 2 * EXPERTS), bf16),
            jax.ShapeDtypeStruct((entries, EXPERTS), bf16),
        ),
        in_specs=[vmem()],
        out_specs=(vmem(), vmem()),
        compiler_params=params(16),
        cost_estimate=cost(1 << 10, 1 << 10),
        name="picks",
    )(ids)


def unpack_kernel(pick_a_ref, pick_b_ref, weight_ref, back_ref, o_ref):
    for n in range(TILES):
        at = n * STRIDE
        slots = back_ref[:, :, at : at + TILE].reshape(2 * EXPERTS, TILE)
        third = back_ref[:, :, at + TILE : at + STRIDE].reshape(EXPERTS, TILE)
        found = contract(pick_a_ref[...], slots, ((1,), (0,))) + contract(
            pick_b_ref[...], third, ((1,), (0,))
        )
        for c in range(TOPK):
            to = c * EH + n * TILE
            part = weight_ref[:, c : c + 1] * found[c * ROWS : (c + 1) * ROWS]
            o_ref[:, to : to + TILE] = part.astype(bf16)


def unpack(pick_a, pick_b, weights, back):
    return pl.pallas_call(
        unpack_kernel,
        out_shape=jax.ShapeDtypeStruct((ROWS, TOPK * EH), bf16),
        in_specs=[vmem()] * 4,
        out_specs=vmem(),
        compiler_params=params(16),
        cost_estimate=cost(2 * 384 * EXPERTS * EH, 2 * MIB),
        name="unpack_rows",
    )(pick_a, pick_b, weights, back)


def query_kernel(rep_ref, nope_ref, comp_ref, from_same_ref, from_cross_ref, other_ref, rise_q_ref,
                 rise_k_ref, down_k_ref, down_q_ref, base_ref, own_ref, same_ref, cross_ref,
                 guest_ref, low_ref, rq_ref, rk_ref, dk_ref, dq_ref):
    step = pl.program_id(0)

    @pl.when(step == 0)
    def _():
        @pl.when(rep_ref[0] == 0)
        def _():
            rq_ref[...] = rise_q_ref[...]
            rk_ref[...] = rise_k_ref[...]
            dk_ref[...] = down_k_ref[...]
            dq_ref[...] = down_q_ref[...]

        @pl.when(rep_ref[0] != 0)
        def _():
            for ref, at, width in (
                (rq_ref, RISE_Q_AT, HCOLS),
                (rk_ref, RISE_K_AT, HCOLS),
                (dk_ref, DOWN_K_AT, LATENT),
                (dq_ref, DOWN_Q_AT, QLORA),
            ):
                ref[:QUARTER] = from_same_ref[:, at : at + width]
                ref[QUARTER : 2 * QUARTER] = from_cross_ref[:, at : at + width]
                at -= RISE_Q_AT
                ref[2 * QUARTER :] = other_ref[:, at : at + width]

        guest_ref[:, :PATH_COLS] = from_same_ref[:, :PATH_COLS]
        guest_ref[:, PATH_COLS:] = from_cross_ref[:, :PATH_COLS]
        down = dq_ref[...]
        comp = (
            comp_ref[...],
            from_same_ref[:, COMP_AT : COMP_AT + QLORA],
            from_cross_ref[:, COMP_AT : COMP_AT + QLORA],
        )
        for k in range(3):
            low = contract(comp[k], down, ((1,), (1,)))
            low_ref[k * ROWS : (k + 1) * ROWS] = low.astype(bf16)

    cols = pl.ds(pl.multiple_of(step * GROUP * NOPE, GROUP * NOPE), GROUP * NOPE)
    path = lax.div(step, 2)
    guest = pl.ds(pl.multiple_of((1 + path) * ROWS, ROWS), ROWS)
    low = jnp.concatenate([low_ref[:ROWS], low_ref[guest]], axis=0)
    nope = jnp.concatenate([nope_ref[...], guest_ref[:, cols]], axis=0)
    delta = contract(low, rq_ref[:, cols], ((1,), (0,)))
    heads = (nope.astype(f32) + delta).astype(bf16)
    rise = rk_ref[:, cols]
    down = dk_ref[...]
    kept = []
    for h in range(GROUP):
        query = heads[:, h * NOPE : (h + 1) * NOPE]
        mixed = contract(query, rise[:, h * NOPE : (h + 1) * NOPE], ((1,), (1,)))
        high = mixed.astype(bf16)
        rest = (mixed - high.astype(f32)).astype(bf16)
        latent = (
            contract(query, base_ref[h], ((1,), (0,)))
            + contract(high, down, ((1,), (0,)))
            + contract(rest, down, ((1,), (0,)))
        )
        own_ref[h] = latent[:ROWS].astype(bf16)
        kept.append(latent[ROWS:].astype(bf16))

    @pl.when(path == 0)
    def _():
        for h in range(GROUP):
            same_ref[h] = kept[h]

    @pl.when(path != 0)
    def _():
        for h in range(GROUP):
            cross_ref[h] = kept[h]


def query_part(rep, nope, comp, from_same, from_cross, other, rise_q, rise_k, down_k, down_q, base):
    steps = HALF // GROUP
    block = (GROUP, ROWS, LATENT)
    return pl.pallas_call(
        query_kernel,
        out_shape=(
            jax.ShapeDtypeStruct((HALF, ROWS, LATENT), bf16),
            jax.ShapeDtypeStruct((HALF // 2, ROWS, LATENT), bf16),
            jax.ShapeDtypeStruct((HALF // 2, ROWS, LATENT), bf16),
        ),
        grid_spec=pltpu.PrefetchScalarGridSpec(
            num_scalar_prefetch=1,
            grid=(steps,),
            in_specs=[
                pl.BlockSpec((ROWS, GROUP * NOPE), lambda g, r: (0, r[0] * steps + g)),
                pl.BlockSpec((ROWS, QLORA), lambda g, r: (0, 0)),
                pl.BlockSpec((ROWS, PAYLOAD), lambda g, r: (0, 0)),
                pl.BlockSpec((ROWS, PAYLOAD), lambda g, r: (0, 0)),
                pl.BlockSpec((2 * QUARTER, PAYLOAD - RISE_Q_AT), lambda g, r: (0, 0)),
                pl.BlockSpec((RANK, HCOLS), lambda g, r: (0, 0)),
                pl.BlockSpec((RANK, HCOLS), lambda g, r: (0, 0)),
                pl.BlockSpec((RANK, LATENT), lambda g, r: (0, 0)),
                pl.BlockSpec((RANK, QLORA), lambda g, r: (0, 0)),
                pl.BlockSpec((GROUP, NOPE, LATENT), lambda g, r: (g, 0, 0)),
            ],
            out_specs=(
                pl.BlockSpec(block, lambda g, r: (g, 0, 0)),
                pl.BlockSpec(block, lambda g, r: (jnp.minimum(g, 1), 0, 0)),
                pl.BlockSpec(block, lambda g, r: (jnp.maximum(g - 2, 0), 0, 0)),
            ),
            scratch_shapes=[
                pltpu.VMEM((ROWS, HCOLS), bf16),
                pltpu.VMEM((3 * ROWS, RANK), bf16),
                pltpu.VMEM((RANK, HCOLS), bf16),
                pltpu.VMEM((RANK, HCOLS), bf16),
                pltpu.VMEM((RANK, LATENT), bf16),
                pltpu.VMEM((RANK, QLORA), bf16),
            ],
        ),
        compiler_params=params(24),
        cost_estimate=cost(20000000000, 1 << 10),
        name="query_latent",
    )(rep, in_hbm(nope), comp, from_same, from_cross, other, *map(in_hbm, (rise_q, rise_k, down_k, down_q, base)))


BATCH = 2
LANES = LATENT // 128


def attend_kernel(lengths_ref, rep_ref, own_ref, same_ref, cross_ref, rope_ref, kv_ref,
                  o_ref, query_ref, done_ref):
    step = pl.program_id(0)

    @pl.when(step == 0)
    def _():
        mine = rep_ref[0] * HALF
        other = HALF - mine
        for h in range(HALF):
            at = pl.multiple_of((mine + h) * ROWS, ROWS)
            value = own_ref[h].astype(f32)
            for j in range(LANES):
                query_ref[j, pl.ds(at, ROWS), :] = value[:, j * 128 : (j + 1) * 128]
        for k, ref in enumerate((same_ref, cross_ref)):
            for h in range(HALF // 2):
                at = pl.multiple_of((other + k * (HALF // 2) + h) * ROWS, ROWS)
                value = ref[h].astype(f32)
                for j in range(LANES):
                    query_ref[j, pl.ds(at, ROWS), :] = value[:, j * 128 : (j + 1) * 128]

    for b in range(BATCH):
        row = step * BATCH + b
        query = jnp.concatenate(
            [query_ref[j, pl.ds(row, HEADS, stride=ROWS), :] for j in range(LANES)], axis=1
        ).astype(bf16)
        kv = kv_ref[b]
        scores = contract(query, kv[:, :LATENT], ((1,), (1,))) + contract(
            rope_ref[b], kv[:, LATENT:], ((1,), (1,))
        )
        scores = scores * (1.0 / (NOPE + ROPE) ** 0.5)
        live = lax.broadcasted_iota(jnp.int32, scores.shape, 1) < lengths_ref[row]
        scores = jnp.where(live, scores, -1e30)
        highest = jnp.max(scores, axis=1, keepdims=True)
        exponent = jnp.where(live, jnp.exp(scores - highest), 0.0)
        weights = (exponent / jnp.sum(exponent, axis=1, keepdims=True)).astype(bf16)
        at = pl.multiple_of(row * HEADS, HEADS)
        latent = contract(weights, kv[:, :LATENT], ((1,), (0,)))
        for j in range(LANES):
            done_ref[j, pl.ds(at, HEADS), :] = latent[:, j * 128 : (j + 1) * 128]

    @pl.when(step == pl.num_programs(0) - 1)
    def _():
        for h in range(HEADS):
            for j in range(LANES):
                at = h * LATENT + j * 128
                o_ref[:, at : at + 128] = done_ref[
                    j, pl.ds(h, ROWS, stride=HEADS), :
                ].astype(bf16)


def attend(lengths, rep, own, same, cross, rope, kv):
    whole = lambda s, *_: (0, 0, 0)
    half = pl.BlockSpec((HALF // 2, ROWS, LATENT), whole)
    return pl.pallas_call(
        attend_kernel,
        out_shape=jax.ShapeDtypeStruct((ROWS, HEADS * LATENT), bf16),
        grid_spec=pltpu.PrefetchScalarGridSpec(
            num_scalar_prefetch=2,
            grid=(ROWS // BATCH,),
            in_specs=[
                pl.BlockSpec((HALF, ROWS, LATENT), whole),
                half,
                half,
                pl.BlockSpec((BATCH, HEADS, ROPE), lambda s, *_: (s, 0, 0)),
                pl.BlockSpec((BATCH, LEN, LATENT + ROPE), lambda s, *_: (s, 0, 0)),
            ],
            out_specs=pl.BlockSpec((ROWS, HEADS * LATENT), lambda s, *_: (0, 0)),
            scratch_shapes=[
                pltpu.VMEM((LANES, HEADS * ROWS, 128), f32),
                pltpu.VMEM((LANES, ROWS * HEADS, 128), f32),
            ],
        ),
        compiler_params=params(40),
        cost_estimate=cost(2 * ROWS * HEADS * LEN * 1088, 6 * MIB, ROWS * HEADS * LEN),
        name="attend_rows",
    )(lengths, rep, own, in_hbm(same), in_hbm(cross), rope, in_hbm(kv))


def on_device(
    query_nope,
    query_rope,
    query_compressed,
    kv_cache,
    cache_lengths,
    key_base,
    query_down,
    query_rise,
    key_down,
    key_rise,
    moe_input,
    expert_ids,
    route_weights,
    expert_gate_up,
):
    rep = lax.axis_index("rep")
    ep_size = lax.axis_size("ep")
    every = [(r, e) for r in range(2) for e in range(ep_size)]
    place = lambda r, e: r * ep_size + e
    to_same = [(place(r, e), place(1 - r, e)) for r, e in every]
    to_cross = [(place(r, e), place(1 - r, e ^ 2)) for r, e in every]
    to_core = [(e, e ^ 1) for e in range(ep_size)]

    factors = (query_rise[0], key_rise[0], key_down[0], query_down[0].T)
    ids = expert_ids.T
    same, cross, mask_a, mask_b = payloads(ids, query_nope, query_compressed, *factors)
    moe_input, same, cross = lax.optimization_barrier((moe_input, same, cross))
    leaving_rows = pack(mask_a, mask_b, moe_input)
    arrived_rows = lax.all_to_all(leaving_rows, AXES, 0, 0, tiled=True)

    from_same = lax.ppermute(same, AXES, to_same)
    from_cross = lax.ppermute(cross, AXES, to_cross)
    half = jnp.concatenate([from_same[:, RISE_Q_AT:], from_cross[:, RISE_Q_AT:]], axis=0)
    other = lax.ppermute(half, "ep", to_core)
    own, same, cross = query_part(
        rep.reshape(1), query_nope, query_compressed, from_same, from_cross, other, *factors, key_base
    )
    same = lax.ppermute(same, AXES, to_same)
    cross = lax.ppermute(cross, AXES, to_cross)
    ids, own = lax.optimization_barrier((ids, own))
    pick_a, pick_b = picks(ids)
    arrived_rows, own, pick_a, pick_b = lax.optimization_barrier(
        (arrived_rows, own, pick_a, pick_b)
    )
    rope = query_rope.reshape(ROWS, HEADS, ROPE)
    activation = expert(arrived_rows, expert_gate_up)
    activation, same, cross = lax.optimization_barrier((activation, same, cross))
    back = lax.all_to_all(activation, AXES, 0, 0, tiled=True)
    attended = attend(cache_lengths, rep.reshape(1), own, same, cross, rope, kv_cache)
    expert_hidden = unpack(pick_a, pick_b, route_weights, back)
    return (attended, expert_hidden)


def solution(mesh):
    both = ("rep", "ep")
    return jax.shard_map(
        on_device,
        mesh=mesh,
        in_specs=(
            P(both, None),
            P(both, None),
            P(both, None),
            P(both, None, None),
            P(both),
            P("rep", None, None),
            P("rep", None, None),
            P("rep", None, None),
            P("rep", None, None),
            P("rep", None, None),
            P(both, None),
            P(both, None),
            P(both, None),
            P(both, None, None),
        ),
        out_specs=(P(both, None), P(both, None)),
        check_vma=False,
    )
```

```python
import functools

import jax
import jax.numpy as jnp
from jax import lax
from jax.experimental import pallas as pl
from jax.experimental.pallas import tpu as pltpu
from jax.sharding import PartitionSpec as P

HEADS = 64
NOPE = 128
ROPE = 64
LATENT = 512
RANK = 64
QLORA = 1536
D = 3584
EH = 1024
TOPK = 8
ROWS = 16
LEN = 192
EXPERTS = 128
HALF = HEADS // 2
HCOLS = HALF * NOPE
GROUP = 8
PATH_COLS = HCOLS // 2
QUARTER = RANK // 4
COMP_AT = PATH_COLS
RISE_Q_AT = COMP_AT + QLORA
RISE_K_AT = RISE_Q_AT + HCOLS
DOWN_K_AT = RISE_K_AT + HCOLS
DOWN_Q_AT = DOWN_K_AT + LATENT
PAYLOAD = DOWN_Q_AT + QLORA
AXES = ("rep", "ep")
MIB = 1 << 20

f32 = jnp.float32
bf16 = jnp.bfloat16


def contract(a, b, dims):
    return lax.dot_general(a, b, (dims, ((), ())), preferred_element_type=f32)


def vmem():
    return pl.BlockSpec(memory_space=pltpu.VMEM)


def in_hbm(x):
    return pltpu.with_memory_space_constraint(x, pltpu.HBM)


def params(mib, **more):
    return pltpu.CompilerParams(vmem_limit_bytes=mib * MIB, **more)


def cost(flops, moved, exps=0):
    return pl.CostEstimate(flops=flops, bytes_accessed=moved, transcendentals=exps)


def named_and_rank(ids, slots, shift):
    expert = lax.broadcasted_iota(jnp.int32, (slots, ROWS), 0)
    if shift:
        expert = lax.shift_right_logical(expert, shift)
    named = jnp.zeros((slots, ROWS), f32)
    for c in range(TOPK):
        named = jnp.where(ids[c : c + 1, :] == expert, 1.0, named)
    above = lax.broadcasted_iota(jnp.int32, (ROWS, ROWS), 0) < lax.broadcasted_iota(
        jnp.int32, (ROWS, ROWS), 1
    )
    rank = contract(named.astype(bf16), above.astype(bf16), ((1,), (0,)))
    return named, rank


def slot_masks(ids):
    named, rank = named_and_rank(ids, 2 * EXPERTS, 1)
    slot = lax.broadcasted_iota(jnp.int32, (2 * EXPERTS, ROWS), 0) & 1
    mask_a = jnp.where(rank == slot.astype(f32), named, 0.0)
    named, rank = named_and_rank(ids, EXPERTS, 0)
    mask_b = jnp.where(rank == 2.0, named, 0.0)
    return mask_a, mask_b


PIECE = 512
PIECES = D // PIECE
PART = 256
TAKEN = (1, 2, 3, 4, 4)
SPAN = PIECE + PIECE // 2
TILE = 256
TILES = EH // TILE
STRIDE = TILE + TILE // 2


def payload_kernel(ids_ref, nope_ref, comp_ref, rise_q_ref, rise_k_ref, down_k_ref, down_q_ref,
                   same_ref, cross_ref, a_ref, b_ref, held_ref, done):
    rep, core = lax.axis_index("rep"), lax.rem(lax.axis_index("ep"), 2)
    named = pltpu.make_async_copy(ids_ref, held_ref, done.at[12])
    named.start()
    copies = []
    for path, target in enumerate((same_ref, cross_ref)):
        at = pl.multiple_of((1 - rep) * HCOLS + path * PATH_COLS, 128)
        rows = pl.ds(pl.multiple_of((core * 2 + path) * QUARTER, QUARTER), QUARTER)
        for source, to, width in (
            (rise_q_ref.at[rows, pl.ds(HCOLS, HCOLS)], RISE_Q_AT, HCOLS),
            (rise_k_ref.at[rows, pl.ds(HCOLS, HCOLS)], RISE_K_AT, HCOLS),
            (nope_ref.at[:, pl.ds(at, PATH_COLS)], 0, PATH_COLS),
            (comp_ref, COMP_AT, QLORA),
            (down_k_ref.at[rows, :], DOWN_K_AT, LATENT),
            (down_q_ref.at[rows, :], DOWN_Q_AT, QLORA),
        ):
            copy = pltpu.make_async_copy(
                source, target.at[:, pl.ds(to, width)], done.at[len(copies)]
            )
            copy.start()
            copies.append(copy)
    named.wait()
    mask_a, mask_b = slot_masks(held_ref[...])
    a_ref[...] = mask_a.astype(bf16)
    b_ref[...] = mask_b.astype(bf16)
    for copy in copies:
        copy.wait()


def payloads(ids, nope, comp, rise_q, rise_k, down_k, down_q):
    hbm = pl.BlockSpec(memory_space=pltpu.HBM)
    return pl.pallas_call(
        payload_kernel,
        out_shape=(
            jax.ShapeDtypeStruct((ROWS, PAYLOAD), bf16),
            jax.ShapeDtypeStruct((ROWS, PAYLOAD), bf16),
            jax.ShapeDtypeStruct((2 * EXPERTS, ROWS), bf16),
            jax.ShapeDtypeStruct((EXPERTS, ROWS), bf16),
        ),
        in_specs=[hbm] * 7,
        out_specs=(vmem(),) * 4,
        scratch_shapes=[pltpu.VMEM((TOPK, ROWS), jnp.int32), pltpu.SemaphoreType.DMA((13,))],
        compiler_params=params(16),
        cost_estimate=cost(1 << 10, 1 << 20),
        name="payloads",
    )(*map(in_hbm, (ids, nope, comp, rise_q, rise_k, down_k, down_q)))


def pack_kernel(a_ref, b_ref, x_ref, o_ref, packed_ref, sent):
    mask_a, mask_b = a_ref[...], b_ref[...]
    copies = []
    for g in range(PIECES):
        x = x_ref[:, g * PIECE : (g + 1) * PIECE]
        at = g * SPAN
        rows = contract(mask_a, x, ((1,), (0,))).astype(bf16)
        packed_ref[:, :, at : at + PIECE] = rows.reshape(EXPERTS, 2, PIECE)
        rows = contract(mask_b, x, ((1,), (0,))).astype(bf16)
        packed_ref[:, :, at + PIECE : at + SPAN] = rows.reshape(EXPERTS, 2, PIECE // 2)
        lanes = pl.ds(at, SPAN)
        copy = pltpu.make_async_copy(
            packed_ref.at[:, :, lanes], o_ref.at[:, :, lanes], sent.at[g]
        )
        copy.start()
        copies.append(copy)
    for copy in copies:
        copy.wait()


def pack(mask_a, mask_b, x):
    shape = (EXPERTS, 2, PIECES * SPAN)
    return pl.pallas_call(
        pack_kernel,
        out_shape=pltpu.HBM(shape, bf16),
        in_specs=[vmem(), vmem(), vmem()],
        out_specs=pl.BlockSpec(memory_space=pltpu.HBM),
        scratch_shapes=[pltpu.VMEM(shape, bf16), pltpu.SemaphoreType.DMA((PIECES,))],
        compiler_params=params(16),
        cost_estimate=cost(2 * 384 * ROWS * D, 3 * MIB),
        name="pack_rows",
    )(mask_a, mask_b, x)


def expert_kernel(x_ref, w_ref, o_ref, xs_ref, held_ref, sum_ref, act_ref, came, left):
    rows, wide = 3 * EXPERTS, 2 * TILE
    copies, leaving = [], []
    for g in range(D // PART):
        part = pl.ds(g * PART, PART)
        copy = pltpu.make_async_copy(w_ref.at[0, part, :], held_ref.at[part, :], came.at[g])
        copy.start()
        copies.append(copy)
    for g in range(PIECES):
        at, to = g * SPAN, slice(g * PIECE, (g + 1) * PIECE)
        xs_ref[: 2 * EXPERTS, to] = x_ref[:, :, at : at + PIECE].reshape(2 * EXPERTS, PIECE)
        xs_ref[2 * EXPERTS :, to] = x_ref[:, :, at + PIECE : at + SPAN].reshape(EXPERTS, PIECE)
    done = 0
    for take in TAKEN[:-1]:
        for g in range(done, done + take):
            copies[g].wait()
        part = slice(done * PART, (done + take) * PART)
        for n in range(2 * EH // wide):
            to = slice(n * wide, (n + 1) * wide)
            term = contract(xs_ref[:, part], held_ref[part, to], ((1,), (0,)))
            sum_ref[:, to] = term if done == 0 else sum_ref[:, to] + term
        done += take
    for g in range(done, D // PART):
        copies[g].wait()
    part = slice(done * PART, D)
    for n in range(TILES):
        both = []
        for k in range(2):
            to = slice(k * EH + n * TILE, k * EH + (n + 1) * TILE)
            term = contract(xs_ref[:, part], held_ref[part, to], ((1,), (0,)))
            both.append(sum_ref[:, to] + term)
        gate, up = both
        act = (gate / (1.0 + jnp.exp(-gate)) * up).astype(bf16)
        at = n * STRIDE
        act_ref[:, :, at : at + TILE] = act[: 2 * EXPERTS].reshape(EXPERTS, 2, TILE)
        act_ref[:, :, at + TILE : at + STRIDE] = act[2 * EXPERTS :].reshape(EXPERTS, 2, TILE // 2)
        lanes = pl.ds(at, STRIDE)
        copy = pltpu.make_async_copy(act_ref.at[:, :, lanes], o_ref.at[:, :, lanes], left.at[n])
        copy.start()
        leaving.append(copy)
    for copy in leaving:
        copy.wait()


def expert(x, w):
    rows = 3 * EXPERTS
    x = pltpu.with_memory_space_constraint(x, pltpu.VMEM)
    return pl.pallas_call(
        expert_kernel,
        out_shape=pltpu.HBM((EXPERTS, 2, TILES * STRIDE), bf16),
        in_specs=[vmem(), pl.BlockSpec(memory_space=pltpu.HBM)],
        out_specs=pl.BlockSpec(memory_space=pltpu.HBM),
        scratch_shapes=[
            pltpu.VMEM((rows, D), bf16),
            pltpu.VMEM((D, 2 * EH), bf16),
            pltpu.VMEM((rows, 2 * EH), f32),
            pltpu.VMEM((EXPERTS, 2, TILES * STRIDE), bf16),
            pltpu.SemaphoreType.DMA((D // PART,)),
            pltpu.SemaphoreType.DMA((TILES,)),
        ],
        compiler_params=params(40),
        cost_estimate=cost(2 * rows * D * 2 * EH, 18 * MIB, rows * EH),
        name="expert_rows",
    )(x, in_hbm(w))


def picks_kernel(ids_ref, a_ref, b_ref):
    ids = ids_ref[...]
    mask_a, mask_b = slot_masks(ids)
    slot_a = lax.shift_right_logical(
        lax.broadcasted_iota(jnp.int32, (2 * EXPERTS, ROWS), 0), 1
    )
    slot_b = lax.broadcasted_iota(jnp.int32, (EXPERTS, ROWS), 0)
    pick_a = [jnp.where(ids[c : c + 1, :] == slot_a, mask_a, 0.0) for c in range(TOPK)]
    pick_b = [jnp.where(ids[c : c + 1, :] == slot_b, mask_b, 0.0) for c in range(TOPK)]
    a_ref[...] = jnp.concatenate(pick_a, axis=1).T.astype(bf16)
    b_ref[...] = jnp.concatenate(pick_b, axis=1).T.astype(bf16)


def picks(ids):
    entries = TOPK * ROWS
    return pl.pallas_call(
        picks_kernel,
        out_shape=(
            jax.ShapeDtypeStruct((entries, 2 * EXPERTS), bf16),
            jax.ShapeDtypeStruct((entries, EXPERTS), bf16),
        ),
        in_specs=[vmem()],
        out_specs=(vmem(), vmem()),
        compiler_params=params(16),
        cost_estimate=cost(1 << 10, 1 << 10),
        name="picks",
    )(ids)


def unpack_kernel(pick_a_ref, pick_b_ref, weight_ref, back_ref, o_ref):
    for n in range(TILES):
        at = n * STRIDE
        slots = back_ref[:, :, at : at + TILE].reshape(2 * EXPERTS, TILE)
        third = back_ref[:, :, at + TILE : at + STRIDE].reshape(EXPERTS, TILE)
        found = contract(pick_a_ref[...], slots, ((1,), (0,))) + contract(
            pick_b_ref[...], third, ((1,), (0,))
        )
        for c in range(TOPK):
            to = c * EH + n * TILE
            part = weight_ref[:, c : c + 1] * found[c * ROWS : (c + 1) * ROWS]
            o_ref[:, to : to + TILE] = part.astype(bf16)


def unpack(pick_a, pick_b, weights, back):
    return pl.pallas_call(
        unpack_kernel,
        out_shape=jax.ShapeDtypeStruct((ROWS, TOPK * EH), bf16),
        in_specs=[vmem()] * 4,
        out_specs=vmem(),
        compiler_params=params(16),
        cost_estimate=cost(2 * 384 * EXPERTS * EH, 2 * MIB),
        name="unpack_rows",
    )(pick_a, pick_b, weights, back)


def query_kernel(rep_ref, nope_ref, comp_ref, from_same_ref, from_cross_ref, other_ref, rise_q_ref,
                 rise_k_ref, down_k_ref, down_q_ref, base_ref, own_ref, same_ref, cross_ref,
                 guest_ref, low_ref, rq_ref, rk_ref, dk_ref, dq_ref):
    step = pl.program_id(0)

    @pl.when(step == 0)
    def _():
        @pl.when(rep_ref[0] == 0)
        def _():
            rq_ref[...] = rise_q_ref[...]
            rk_ref[...] = rise_k_ref[...]
            dk_ref[...] = down_k_ref[...]
            dq_ref[...] = down_q_ref[...]

        @pl.when(rep_ref[0] != 0)
        def _():
            for ref, at, width in (
                (rq_ref, RISE_Q_AT, HCOLS),
                (rk_ref, RISE_K_AT, HCOLS),
                (dk_ref, DOWN_K_AT, LATENT),
                (dq_ref, DOWN_Q_AT, QLORA),
            ):
                ref[:QUARTER] = from_same_ref[:, at : at + width]
                ref[QUARTER : 2 * QUARTER] = from_cross_ref[:, at : at + width]
                at -= RISE_Q_AT
                ref[2 * QUARTER :] = other_ref[:, at : at + width]

        guest_ref[:, :PATH_COLS] = from_same_ref[:, :PATH_COLS]
        guest_ref[:, PATH_COLS:] = from_cross_ref[:, :PATH_COLS]
        down = dq_ref[...]
        comp = (
            comp_ref[...],
            from_same_ref[:, COMP_AT : COMP_AT + QLORA],
            from_cross_ref[:, COMP_AT : COMP_AT + QLORA],
        )
        for k in range(3):
            low = contract(comp[k], down, ((1,), (1,)))
            low_ref[k * ROWS : (k + 1) * ROWS] = low.astype(bf16)

    cols = pl.ds(pl.multiple_of(step * GROUP * NOPE, GROUP * NOPE), GROUP * NOPE)
    path = lax.div(step, 2)
    guest = pl.ds(pl.multiple_of((1 + path) * ROWS, ROWS), ROWS)
    low = jnp.concatenate([low_ref[:ROWS], low_ref[guest]], axis=0)
    nope = jnp.concatenate([nope_ref[...], guest_ref[:, cols]], axis=0)
    delta = contract(low, rq_ref[:, cols], ((1,), (0,)))
    heads = (nope.astype(f32) + delta).astype(bf16)
    rise = rk_ref[:, cols]
    down = dk_ref[...]
    kept = []
    for h in range(GROUP):
        query = heads[:, h * NOPE : (h + 1) * NOPE]
        mixed = contract(query, rise[:, h * NOPE : (h + 1) * NOPE], ((1,), (1,)))
        high = mixed.astype(bf16)
        rest = (mixed - high.astype(f32)).astype(bf16)
        latent = (
            contract(query, base_ref[h], ((1,), (0,)))
            + contract(high, down, ((1,), (0,)))
            + contract(rest, down, ((1,), (0,)))
        )
        own_ref[h] = latent[:ROWS].astype(bf16)
        kept.append(latent[ROWS:].astype(bf16))

    @pl.when(path == 0)
    def _():
        for h in range(GROUP):
            same_ref[h] = kept[h]

    @pl.when(path != 0)
    def _():
        for h in range(GROUP):
            cross_ref[h] = kept[h]


def query_part(rep, nope, comp, from_same, from_cross, other, rise_q, rise_k, down_k, down_q, base):
    steps = HALF // GROUP
    block = (GROUP, ROWS, LATENT)
    return pl.pallas_call(
        query_kernel,
        out_shape=(
            jax.ShapeDtypeStruct((HALF, ROWS, LATENT), bf16),
            jax.ShapeDtypeStruct((HALF // 2, ROWS, LATENT), bf16),
            jax.ShapeDtypeStruct((HALF // 2, ROWS, LATENT), bf16),
        ),
        grid_spec=pltpu.PrefetchScalarGridSpec(
            num_scalar_prefetch=1,
            grid=(steps,),
            in_specs=[
                pl.BlockSpec((ROWS, GROUP * NOPE), lambda g, r: (0, r[0] * steps + g)),
                pl.BlockSpec((ROWS, QLORA), lambda g, r: (0, 0)),
                pl.BlockSpec((ROWS, PAYLOAD), lambda g, r: (0, 0)),
                pl.BlockSpec((ROWS, PAYLOAD), lambda g, r: (0, 0)),
                pl.BlockSpec((2 * QUARTER, PAYLOAD - RISE_Q_AT), lambda g, r: (0, 0)),
                pl.BlockSpec((RANK, HCOLS), lambda g, r: (0, 0)),
                pl.BlockSpec((RANK, HCOLS), lambda g, r: (0, 0)),
                pl.BlockSpec((RANK, LATENT), lambda g, r: (0, 0)),
                pl.BlockSpec((RANK, QLORA), lambda g, r: (0, 0)),
                pl.BlockSpec((GROUP, NOPE, LATENT), lambda g, r: (g, 0, 0)),
            ],
            out_specs=(
                pl.BlockSpec(block, lambda g, r: (g, 0, 0)),
                pl.BlockSpec(block, lambda g, r: (jnp.minimum(g, 1), 0, 0)),
                pl.BlockSpec(block, lambda g, r: (jnp.maximum(g - 2, 0), 0, 0)),
            ),
            scratch_shapes=[
                pltpu.VMEM((ROWS, HCOLS), bf16),
                pltpu.VMEM((3 * ROWS, RANK), bf16),
                pltpu.VMEM((RANK, HCOLS), bf16),
                pltpu.VMEM((RANK, HCOLS), bf16),
                pltpu.VMEM((RANK, LATENT), bf16),
                pltpu.VMEM((RANK, QLORA), bf16),
            ],
        ),
        compiler_params=params(24),
        cost_estimate=cost(20000000000, 1 << 10),
        name="query_latent",
    )(rep, in_hbm(nope), comp, from_same, from_cross, other, *map(in_hbm, (rise_q, rise_k, down_k, down_q, base)))


BATCH = 2
LANES = LATENT // 128


def attend_kernel(lengths_ref, rep_ref, own_ref, same_ref, cross_ref, rope_ref, kv_ref,
                  o_ref, query_ref, done_ref):
    step = pl.program_id(0)

    @pl.when(step == 0)
    def _():
        mine = rep_ref[0] * HALF
        other = HALF - mine
        for h in range(HALF):
            at = pl.multiple_of((mine + h) * ROWS, ROWS)
            value = own_ref[h].astype(f32)
            for j in range(LANES):
                query_ref[j, pl.ds(at, ROWS), :] = value[:, j * 128 : (j + 1) * 128]
        for k, ref in enumerate((same_ref, cross_ref)):
            for h in range(HALF // 2):
                at = pl.multiple_of((other + k * (HALF // 2) + h) * ROWS, ROWS)
                value = ref[h].astype(f32)
                for j in range(LANES):
                    query_ref[j, pl.ds(at, ROWS), :] = value[:, j * 128 : (j + 1) * 128]

    for b in range(BATCH):
        row = step * BATCH + b
        query = jnp.concatenate(
            [query_ref[j, pl.ds(row, HEADS, stride=ROWS), :] for j in range(LANES)], axis=1
        ).astype(bf16)
        kv = kv_ref[b]
        scores = contract(query, kv[:, :LATENT], ((1,), (1,))) + contract(
            rope_ref[b], kv[:, LATENT:], ((1,), (1,))
        )
        scores = scores * (1.0 / (NOPE + ROPE) ** 0.5)
        live = lax.broadcasted_iota(jnp.int32, scores.shape, 1) < lengths_ref[row]
        scores = jnp.where(live, scores, -1e30)
        highest = jnp.max(scores, axis=1, keepdims=True)
        exponent = jnp.where(live, jnp.exp(scores - highest), 0.0)
        weights = (exponent / jnp.sum(exponent, axis=1, keepdims=True)).astype(bf16)
        at = pl.multiple_of(row * HEADS, HEADS)
        latent = contract(weights, kv[:, :LATENT], ((1,), (0,)))
        for j in range(LANES):
            done_ref[j, pl.ds(at, HEADS), :] = latent[:, j * 128 : (j + 1) * 128]

    @pl.when(step == pl.num_programs(0) - 1)
    def _():
        for h in range(HEADS):
            for j in range(LANES):
                at = h * LATENT + j * 128
                o_ref[:, at : at + 128] = done_ref[
                    j, pl.ds(h, ROWS, stride=HEADS), :
                ].astype(bf16)


def attend(lengths, rep, own, same, cross, rope, kv):
    whole = lambda s, *_: (0, 0, 0)
    half = pl.BlockSpec((HALF // 2, ROWS, LATENT), whole)
    return pl.pallas_call(
        attend_kernel,
        out_shape=jax.ShapeDtypeStruct((ROWS, HEADS * LATENT), bf16),
        grid_spec=pltpu.PrefetchScalarGridSpec(
            num_scalar_prefetch=2,
            grid=(ROWS // BATCH,),
            in_specs=[
                pl.BlockSpec((HALF, ROWS, LATENT), whole),
                half,
                half,
                pl.BlockSpec((BATCH, HEADS, ROPE), lambda s, *_: (s, 0, 0)),
                pl.BlockSpec((BATCH, LEN, LATENT + ROPE), lambda s, *_: (s, 0, 0)),
            ],
            out_specs=pl.BlockSpec((ROWS, HEADS * LATENT), lambda s, *_: (0, 0)),
            scratch_shapes=[
                pltpu.VMEM((LANES, HEADS * ROWS, 128), f32),
                pltpu.VMEM((LANES, ROWS * HEADS, 128), f32),
            ],
        ),
        compiler_params=params(40),
        cost_estimate=cost(2 * ROWS * HEADS * LEN * 1088, 6 * MIB, ROWS * HEADS * LEN),
        name="attend_rows",
    )(lengths, rep, own, in_hbm(same), in_hbm(cross), rope, in_hbm(kv))


def on_device(
    query_nope,
    query_rope,
    query_compressed,
    kv_cache,
    cache_lengths,
    key_base,
    query_down,
    query_rise,
    key_down,
    key_rise,
    moe_input,
    expert_ids,
    route_weights,
    expert_gate_up,
):
    rep = lax.axis_index("rep")
    ep_size = lax.axis_size("ep")
    every = [(r, e) for r in range(2) for e in range(ep_size)]
    place = lambda r, e: r * ep_size + e
    to_same = [(place(r, e), place(1 - r, e)) for r, e in every]
    to_cross = [(place(r, e), place(1 - r, e ^ 2)) for r, e in every]
    to_core = [(e, e ^ 1) for e in range(ep_size)]

    factors = (query_rise[0], key_rise[0], key_down[0], query_down[0].T)
    ids = expert_ids.T
    same, cross, mask_a, mask_b = payloads(ids, query_nope, query_compressed, *factors)
    moe_input, same, cross = lax.optimization_barrier((moe_input, same, cross))
    leaving_rows = pack(mask_a, mask_b, moe_input)
    arrived_rows = lax.all_to_all(leaving_rows, AXES, 0, 0, tiled=True)

    from_same = lax.ppermute(same, AXES, to_same)
    from_cross = lax.ppermute(cross, AXES, to_cross)
    half = jnp.concatenate([from_same[:, RISE_Q_AT:], from_cross[:, RISE_Q_AT:]], axis=0)
    other = lax.ppermute(half, "ep", to_core)
    own, same, cross = query_part(
        rep.reshape(1), query_nope, query_compressed, from_same, from_cross, other, *factors, key_base
    )
    same = lax.ppermute(same, AXES, to_same)
    cross = lax.ppermute(cross, AXES, to_cross)
    ids, own = lax.optimization_barrier((ids, own))
    pick_a, pick_b = picks(ids)
    arrived_rows, own, pick_a, pick_b = lax.optimization_barrier(
        (arrived_rows, own, pick_a, pick_b)
    )
    rope = query_rope.reshape(ROWS, HEADS, ROPE)
    activation = expert(arrived_rows, expert_gate_up)
    activation, same, cross = lax.optimization_barrier((activation, same, cross))
    back = lax.all_to_all(activation, AXES, 0, 0, tiled=True)
    attended = attend(cache_lengths, rep.reshape(1), own, same, cross, rope, kv_cache)
    expert_hidden = unpack(pick_a, pick_b, route_weights, back)
    return (attended, expert_hidden)


def solution(mesh):
    both = ("rep", "ep")
    return jax.shard_map(
        on_device,
        mesh=mesh,
        in_specs=(
            P(both, None),
            P(both, None),
            P(both, None),
            P(both, None, None),
            P(both),
            P("rep", None, None),
            P("rep", None, None),
            P("rep", None, None),
            P("rep", None, None),
            P("rep", None, None),
            P(both, None),
            P(both, None),
            P(both, None),
            P(both, None, None),
        ),
        out_specs=(P(both, None), P(both, None)),
        check_vma=False,
    )
```

```python
import functools

import jax
import jax.numpy as jnp
from jax import lax
from jax.experimental import pallas as pl
from jax.experimental.pallas import tpu as pltpu
from jax.sharding import PartitionSpec as P

HEADS = 64
NOPE = 128
ROPE = 64
LATENT = 512
RANK = 64
QLORA = 1536
D = 3584
EH = 1024
TOPK = 8
ROWS = 16
LEN = 192
EXPERTS = 128
HALF = HEADS // 2
HCOLS = HALF * NOPE
GROUP = 8
PATH_COLS = HCOLS // 2
QUARTER = RANK // 4
COMP_AT = PATH_COLS
RISE_Q_AT = COMP_AT + QLORA
RISE_K_AT = RISE_Q_AT + HCOLS
DOWN_K_AT = RISE_K_AT + HCOLS
DOWN_Q_AT = DOWN_K_AT + LATENT
PAYLOAD = DOWN_Q_AT + QLORA
AXES = ("rep", "ep")
MIB = 1 << 20

f32 = jnp.float32
bf16 = jnp.bfloat16


def contract(a, b, dims):
    return lax.dot_general(a, b, (dims, ((), ())), preferred_element_type=f32)


def vmem():
    return pl.BlockSpec(memory_space=pltpu.VMEM)


def in_hbm(x):
    return pltpu.with_memory_space_constraint(x, pltpu.HBM)


def params(mib, **more):
    return pltpu.CompilerParams(vmem_limit_bytes=mib * MIB, **more)


def cost(flops, moved, exps=0):
    return pl.CostEstimate(flops=flops, bytes_accessed=moved, transcendentals=exps)


def named_and_rank(ids, slots, shift):
    expert = lax.broadcasted_iota(jnp.int32, (slots, ROWS), 0)
    if shift:
        expert = lax.shift_right_logical(expert, shift)
    named = jnp.zeros((slots, ROWS), f32)
    for c in range(TOPK):
        named = jnp.where(ids[c : c + 1, :] == expert, 1.0, named)
    above = lax.broadcasted_iota(jnp.int32, (ROWS, ROWS), 0) < lax.broadcasted_iota(
        jnp.int32, (ROWS, ROWS), 1
    )
    rank = contract(named.astype(bf16), above.astype(bf16), ((1,), (0,)))
    return named, rank


def slot_masks(ids):
    named, rank = named_and_rank(ids, 2 * EXPERTS, 1)
    slot = lax.broadcasted_iota(jnp.int32, (2 * EXPERTS, ROWS), 0) & 1
    mask_a = jnp.where(rank == slot.astype(f32), named, 0.0)
    named, rank = named_and_rank(ids, EXPERTS, 0)
    mask_b = jnp.where(rank == 2.0, named, 0.0)
    return mask_a, mask_b


PIECE = 512
PIECES = D // PIECE
TAKEN = (1, 1, 2, 2, 1)
SPAN = PIECE + PIECE // 2
TILE = 256
TILES = EH // TILE
STRIDE = TILE + TILE // 2


def payload_kernel(ids_ref, nope_ref, comp_ref, rise_q_ref, rise_k_ref, down_k_ref, down_q_ref,
                   same_ref, cross_ref, a_ref, b_ref, held_ref, done):
    rep, core = lax.axis_index("rep"), lax.rem(lax.axis_index("ep"), 2)
    named = pltpu.make_async_copy(ids_ref, held_ref, done.at[12])
    named.start()
    copies = []
    for path, target in enumerate((same_ref, cross_ref)):
        at = pl.multiple_of((1 - rep) * HCOLS + path * PATH_COLS, 128)
        rows = pl.ds(pl.multiple_of((core * 2 + path) * QUARTER, QUARTER), QUARTER)
        for source, to, width in (
            (rise_q_ref.at[rows, pl.ds(HCOLS, HCOLS)], RISE_Q_AT, HCOLS),
            (rise_k_ref.at[rows, pl.ds(HCOLS, HCOLS)], RISE_K_AT, HCOLS),
            (nope_ref.at[:, pl.ds(at, PATH_COLS)], 0, PATH_COLS),
            (comp_ref, COMP_AT, QLORA),
            (down_k_ref.at[rows, :], DOWN_K_AT, LATENT),
            (down_q_ref.at[rows, :], DOWN_Q_AT, QLORA),
        ):
            copy = pltpu.make_async_copy(
                source, target.at[:, pl.ds(to, width)], done.at[len(copies)]
            )
            copy.start()
            copies.append(copy)
    named.wait()
    mask_a, mask_b = slot_masks(held_ref[...])
    a_ref[...] = mask_a.astype(bf16)
    b_ref[...] = mask_b.astype(bf16)
    for copy in copies:
        copy.wait()


def payloads(ids, nope, comp, rise_q, rise_k, down_k, down_q):
    hbm = pl.BlockSpec(memory_space=pltpu.HBM)
    return pl.pallas_call(
        payload_kernel,
        out_shape=(
            jax.ShapeDtypeStruct((ROWS, PAYLOAD), bf16),
            jax.ShapeDtypeStruct((ROWS, PAYLOAD), bf16),
            jax.ShapeDtypeStruct((2 * EXPERTS, ROWS), bf16),
            jax.ShapeDtypeStruct((EXPERTS, ROWS), bf16),
        ),
        in_specs=[hbm] * 7,
        out_specs=(vmem(),) * 4,
        scratch_shapes=[pltpu.VMEM((TOPK, ROWS), jnp.int32), pltpu.SemaphoreType.DMA((13,))],
        compiler_params=params(16),
        cost_estimate=cost(1 << 10, 1 << 20),
        name="payloads",
    )(*map(in_hbm, (ids, nope, comp, rise_q, rise_k, down_k, down_q)))


def pack_kernel(a_ref, b_ref, x_ref, o_ref, packed_ref, sent):
    mask_a, mask_b = a_ref[...], b_ref[...]
    copies = []
    for g in range(PIECES):
        x = x_ref[:, g * PIECE : (g + 1) * PIECE]
        at = g * SPAN
        rows = contract(mask_a, x, ((1,), (0,))).astype(bf16)
        packed_ref[:, :, at : at + PIECE] = rows.reshape(EXPERTS, 2, PIECE)
        rows = contract(mask_b, x, ((1,), (0,))).astype(bf16)
        packed_ref[:, :, at + PIECE : at + SPAN] = rows.reshape(EXPERTS, 2, PIECE // 2)
        lanes = pl.ds(at, SPAN)
        copy = pltpu.make_async_copy(
            packed_ref.at[:, :, lanes], o_ref.at[:, :, lanes], sent.at[g]
        )
        copy.start()
        copies.append(copy)
    for copy in copies:
        copy.wait()


def pack(mask_a, mask_b, x):
    shape = (EXPERTS, 2, PIECES * SPAN)
    return pl.pallas_call(
        pack_kernel,
        out_shape=pltpu.HBM(shape, bf16),
        in_specs=[vmem(), vmem(), vmem()],
        out_specs=pl.BlockSpec(memory_space=pltpu.HBM),
        scratch_shapes=[pltpu.VMEM(shape, bf16), pltpu.SemaphoreType.DMA((PIECES,))],
        compiler_params=params(16),
        cost_estimate=cost(2 * 384 * ROWS * D, 3 * MIB),
        name="pack_rows",
    )(mask_a, mask_b, x)


def expert_kernel(x_ref, w_ref, o_ref, xs_ref, held_ref, sum_ref, act_ref, came, left):
    rows, wide = 3 * EXPERTS, 2 * TILE
    copies, leaving = [], []
    for g in range(PIECES):
        part = pl.ds(g * PIECE, PIECE)
        copy = pltpu.make_async_copy(w_ref.at[0, part, :], held_ref.at[part, :], came.at[g])
        copy.start()
        copies.append(copy)
    for g in range(PIECES):
        at, to = g * SPAN, slice(g * PIECE, (g + 1) * PIECE)
        xs_ref[: 2 * EXPERTS, to] = x_ref[:, :, at : at + PIECE].reshape(2 * EXPERTS, PIECE)
        xs_ref[2 * EXPERTS :, to] = x_ref[:, :, at + PIECE : at + SPAN].reshape(EXPERTS, PIECE)
    done = 0
    for take in TAKEN[:-1]:
        for g in range(done, done + take):
            copies[g].wait()
        part = slice(done * PIECE, (done + take) * PIECE)
        for n in range(2 * EH // wide):
            to = slice(n * wide, (n + 1) * wide)
            term = contract(xs_ref[:, part], held_ref[part, to], ((1,), (0,)))
            sum_ref[:, to] = term if done == 0 else sum_ref[:, to] + term
        done += take
    for g in range(done, PIECES):
        copies[g].wait()
    part = slice(done * PIECE, D)
    for n in range(TILES):
        both = []
        for k in range(2):
            to = slice(k * EH + n * TILE, k * EH + (n + 1) * TILE)
            term = contract(xs_ref[:, part], held_ref[part, to], ((1,), (0,)))
            both.append(sum_ref[:, to] + term)
        gate, up = both
        act = (gate / (1.0 + jnp.exp(-gate)) * up).astype(bf16)
        at = n * STRIDE
        act_ref[:, :, at : at + TILE] = act[: 2 * EXPERTS].reshape(EXPERTS, 2, TILE)
        act_ref[:, :, at + TILE : at + STRIDE] = act[2 * EXPERTS :].reshape(EXPERTS, 2, TILE // 2)
        lanes = pl.ds(at, STRIDE)
        copy = pltpu.make_async_copy(act_ref.at[:, :, lanes], o_ref.at[:, :, lanes], left.at[n])
        copy.start()
        leaving.append(copy)
    for copy in leaving:
        copy.wait()


def expert(x, w):
    rows = 3 * EXPERTS
    x = pltpu.with_memory_space_constraint(x, pltpu.VMEM)
    return pl.pallas_call(
        expert_kernel,
        out_shape=pltpu.HBM((EXPERTS, 2, TILES * STRIDE), bf16),
        in_specs=[vmem(), pl.BlockSpec(memory_space=pltpu.HBM)],
        out_specs=pl.BlockSpec(memory_space=pltpu.HBM),
        scratch_shapes=[
            pltpu.VMEM((rows, D), bf16),
            pltpu.VMEM((D, 2 * EH), bf16),
            pltpu.VMEM((rows, 2 * EH), f32),
            pltpu.VMEM((EXPERTS, 2, TILES * STRIDE), bf16),
            pltpu.SemaphoreType.DMA((PIECES,)),
            pltpu.SemaphoreType.DMA((TILES,)),
        ],
        compiler_params=params(40),
        cost_estimate=cost(2 * rows * D * 2 * EH, 18 * MIB, rows * EH),
        name="expert_rows",
    )(x, in_hbm(w))


def picks_kernel(ids_ref, a_ref, b_ref):
    ids = ids_ref[...]
    mask_a, mask_b = slot_masks(ids)
    slot_a = lax.shift_right_logical(
        lax.broadcasted_iota(jnp.int32, (2 * EXPERTS, ROWS), 0), 1
    )
    slot_b = lax.broadcasted_iota(jnp.int32, (EXPERTS, ROWS), 0)
    pick_a = [jnp.where(ids[c : c + 1, :] == slot_a, mask_a, 0.0) for c in range(TOPK)]
    pick_b = [jnp.where(ids[c : c + 1, :] == slot_b, mask_b, 0.0) for c in range(TOPK)]
    a_ref[...] = jnp.concatenate(pick_a, axis=1).T.astype(bf16)
    b_ref[...] = jnp.concatenate(pick_b, axis=1).T.astype(bf16)


def picks(ids):
    entries = TOPK * ROWS
    return pl.pallas_call(
        picks_kernel,
        out_shape=(
            jax.ShapeDtypeStruct((entries, 2 * EXPERTS), bf16),
            jax.ShapeDtypeStruct((entries, EXPERTS), bf16),
        ),
        in_specs=[vmem()],
        out_specs=(vmem(), vmem()),
        compiler_params=params(16),
        cost_estimate=cost(1 << 10, 1 << 10),
        name="picks",
    )(ids)


def unpack_kernel(pick_a_ref, pick_b_ref, weight_ref, back_ref, o_ref):
    for n in range(TILES):
        at = n * STRIDE
        slots = back_ref[:, :, at : at + TILE].reshape(2 * EXPERTS, TILE)
        third = back_ref[:, :, at + TILE : at + STRIDE].reshape(EXPERTS, TILE)
        found = contract(pick_a_ref[...], slots, ((1,), (0,))) + contract(
            pick_b_ref[...], third, ((1,), (0,))
        )
        for c in range(TOPK):
            to = c * EH + n * TILE
            part = weight_ref[:, c : c + 1] * found[c * ROWS : (c + 1) * ROWS]
            o_ref[:, to : to + TILE] = part.astype(bf16)


def unpack(pick_a, pick_b, weights, back):
    return pl.pallas_call(
        unpack_kernel,
        out_shape=jax.ShapeDtypeStruct((ROWS, TOPK * EH), bf16),
        in_specs=[vmem()] * 4,
        out_specs=vmem(),
        compiler_params=params(16),
        cost_estimate=cost(2 * 384 * EXPERTS * EH, 2 * MIB),
        name="unpack_rows",
    )(pick_a, pick_b, weights, back)


def query_kernel(rep_ref, nope_ref, comp_ref, from_same_ref, from_cross_ref, other_ref, rise_q_ref,
                 rise_k_ref, down_k_ref, down_q_ref, base_ref, own_ref, same_ref, cross_ref,
                 guest_ref, low_ref, rq_ref, rk_ref, dk_ref, dq_ref):
    step = pl.program_id(0)

    @pl.when(step == 0)
    def _():
        @pl.when(rep_ref[0] == 0)
        def _():
            rq_ref[...] = rise_q_ref[...]
            rk_ref[...] = rise_k_ref[...]
            dk_ref[...] = down_k_ref[...]
            dq_ref[...] = down_q_ref[...]

        @pl.when(rep_ref[0] != 0)
        def _():
            for ref, at, width in (
                (rq_ref, RISE_Q_AT, HCOLS),
                (rk_ref, RISE_K_AT, HCOLS),
                (dk_ref, DOWN_K_AT, LATENT),
                (dq_ref, DOWN_Q_AT, QLORA),
            ):
                ref[:QUARTER] = from_same_ref[:, at : at + width]
                ref[QUARTER : 2 * QUARTER] = from_cross_ref[:, at : at + width]
                at -= RISE_Q_AT
                ref[2 * QUARTER :] = other_ref[:, at : at + width]

        guest_ref[:, :PATH_COLS] = from_same_ref[:, :PATH_COLS]
        guest_ref[:, PATH_COLS:] = from_cross_ref[:, :PATH_COLS]
        down = dq_ref[...]
        comp = (
            comp_ref[...],
            from_same_ref[:, COMP_AT : COMP_AT + QLORA],
            from_cross_ref[:, COMP_AT : COMP_AT + QLORA],
        )
        for k in range(3):
            low = contract(comp[k], down, ((1,), (1,)))
            low_ref[k * ROWS : (k + 1) * ROWS] = low.astype(bf16)

    cols = pl.ds(pl.multiple_of(step * GROUP * NOPE, GROUP * NOPE), GROUP * NOPE)
    path = lax.div(step, 2)
    guest = pl.ds(pl.multiple_of((1 + path) * ROWS, ROWS), ROWS)
    low = jnp.concatenate([low_ref[:ROWS], low_ref[guest]], axis=0)
    nope = jnp.concatenate([nope_ref[...], guest_ref[:, cols]], axis=0)
    delta = contract(low, rq_ref[:, cols], ((1,), (0,)))
    heads = (nope.astype(f32) + delta).astype(bf16)
    rise = rk_ref[:, cols]
    down = dk_ref[...]
    kept = []
    for h in range(GROUP):
        query = heads[:, h * NOPE : (h + 1) * NOPE]
        mixed = contract(query, rise[:, h * NOPE : (h + 1) * NOPE], ((1,), (1,)))
        high = mixed.astype(bf16)
        rest = (mixed - high.astype(f32)).astype(bf16)
        latent = (
            contract(query, base_ref[h], ((1,), (0,)))
            + contract(high, down, ((1,), (0,)))
            + contract(rest, down, ((1,), (0,)))
        )
        own_ref[h] = latent[:ROWS].astype(bf16)
        kept.append(latent[ROWS:].astype(bf16))

    @pl.when(path == 0)
    def _():
        for h in range(GROUP):
            same_ref[h] = kept[h]

    @pl.when(path != 0)
    def _():
        for h in range(GROUP):
            cross_ref[h] = kept[h]


def query_part(rep, nope, comp, from_same, from_cross, other, rise_q, rise_k, down_k, down_q, base):
    steps = HALF // GROUP
    block = (GROUP, ROWS, LATENT)
    return pl.pallas_call(
        query_kernel,
        out_shape=(
            jax.ShapeDtypeStruct((HALF, ROWS, LATENT), bf16),
            jax.ShapeDtypeStruct((HALF // 2, ROWS, LATENT), bf16),
            jax.ShapeDtypeStruct((HALF // 2, ROWS, LATENT), bf16),
        ),
        grid_spec=pltpu.PrefetchScalarGridSpec(
            num_scalar_prefetch=1,
            grid=(steps,),
            in_specs=[
                pl.BlockSpec((ROWS, GROUP * NOPE), lambda g, r: (0, r[0] * steps + g)),
                pl.BlockSpec((ROWS, QLORA), lambda g, r: (0, 0)),
                pl.BlockSpec((ROWS, PAYLOAD), lambda g, r: (0, 0)),
                pl.BlockSpec((ROWS, PAYLOAD), lambda g, r: (0, 0)),
                pl.BlockSpec((2 * QUARTER, PAYLOAD - RISE_Q_AT), lambda g, r: (0, 0)),
                pl.BlockSpec((RANK, HCOLS), lambda g, r: (0, 0)),
                pl.BlockSpec((RANK, HCOLS), lambda g, r: (0, 0)),
                pl.BlockSpec((RANK, LATENT), lambda g, r: (0, 0)),
                pl.BlockSpec((RANK, QLORA), lambda g, r: (0, 0)),
                pl.BlockSpec((GROUP, NOPE, LATENT), lambda g, r: (g, 0, 0)),
            ],
            out_specs=(
                pl.BlockSpec(block, lambda g, r: (g, 0, 0)),
                pl.BlockSpec(block, lambda g, r: (jnp.minimum(g, 1), 0, 0)),
                pl.BlockSpec(block, lambda g, r: (jnp.maximum(g - 2, 0), 0, 0)),
            ),
            scratch_shapes=[
                pltpu.VMEM((ROWS, HCOLS), bf16),
                pltpu.VMEM((3 * ROWS, RANK), bf16),
                pltpu.VMEM((RANK, HCOLS), bf16),
                pltpu.VMEM((RANK, HCOLS), bf16),
                pltpu.VMEM((RANK, LATENT), bf16),
                pltpu.VMEM((RANK, QLORA), bf16),
            ],
        ),
        compiler_params=params(24),
        cost_estimate=cost(20000000000, 1 << 10),
        name="query_latent",
    )(rep, in_hbm(nope), comp, from_same, from_cross, other, *map(in_hbm, (rise_q, rise_k, down_k, down_q, base)))


BATCH = 2
LANES = LATENT // 128


def attend_kernel(lengths_ref, rep_ref, own_ref, same_ref, cross_ref, rope_ref, kv_ref,
                  o_ref, query_ref, done_ref):
    step = pl.program_id(0)

    @pl.when(step == 0)
    def _():
        mine = rep_ref[0] * HALF
        other = HALF - mine
        for h in range(HALF):
            at = pl.multiple_of((mine + h) * ROWS, ROWS)
            value = own_ref[h].astype(f32)
            for j in range(LANES):
                query_ref[j, pl.ds(at, ROWS), :] = value[:, j * 128 : (j + 1) * 128]
        for k, ref in enumerate((same_ref, cross_ref)):
            for h in range(HALF // 2):
                at = pl.multiple_of((other + k * (HALF // 2) + h) * ROWS, ROWS)
                value = ref[h].astype(f32)
                for j in range(LANES):
                    query_ref[j, pl.ds(at, ROWS), :] = value[:, j * 128 : (j + 1) * 128]

    for b in range(BATCH):
        row = step * BATCH + b
        query = jnp.concatenate(
            [query_ref[j, pl.ds(row, HEADS, stride=ROWS), :] for j in range(LANES)], axis=1
        ).astype(bf16)
        kv = kv_ref[b]
        scores = contract(query, kv[:, :LATENT], ((1,), (1,))) + contract(
            rope_ref[b], kv[:, LATENT:], ((1,), (1,))
        )
        scores = scores * (1.0 / (NOPE + ROPE) ** 0.5)
        live = lax.broadcasted_iota(jnp.int32, scores.shape, 1) < lengths_ref[row]
        scores = jnp.where(live, scores, -1e30)
        highest = jnp.max(scores, axis=1, keepdims=True)
        exponent = jnp.where(live, jnp.exp(scores - highest), 0.0)
        weights = (exponent / jnp.sum(exponent, axis=1, keepdims=True)).astype(bf16)
        at = pl.multiple_of(row * HEADS, HEADS)
        latent = contract(weights, kv[:, :LATENT], ((1,), (0,)))
        for j in range(LANES):
            done_ref[j, pl.ds(at, HEADS), :] = latent[:, j * 128 : (j + 1) * 128]

    @pl.when(step == pl.num_programs(0) - 1)
    def _():
        for h in range(HEADS):
            for j in range(LANES):
                at = h * LATENT + j * 128
                o_ref[:, at : at + 128] = done_ref[
                    j, pl.ds(h, ROWS, stride=HEADS), :
                ].astype(bf16)


def attend(lengths, rep, own, same, cross, rope, kv):
    whole = lambda s, *_: (0, 0, 0)
    half = pl.BlockSpec((HALF // 2, ROWS, LATENT), whole)
    return pl.pallas_call(
        attend_kernel,
        out_shape=jax.ShapeDtypeStruct((ROWS, HEADS * LATENT), bf16),
        grid_spec=pltpu.PrefetchScalarGridSpec(
            num_scalar_prefetch=2,
            grid=(ROWS // BATCH,),
            in_specs=[
                pl.BlockSpec((HALF, ROWS, LATENT), whole),
                half,
                half,
                pl.BlockSpec((BATCH, HEADS, ROPE), lambda s, *_: (s, 0, 0)),
                pl.BlockSpec((BATCH, LEN, LATENT + ROPE), lambda s, *_: (s, 0, 0)),
            ],
            out_specs=pl.BlockSpec((ROWS, HEADS * LATENT), lambda s, *_: (0, 0)),
            scratch_shapes=[
                pltpu.VMEM((LANES, (HEADS + 1) * ROWS, 128), f32),
                pltpu.VMEM((LANES, (ROWS + 1) * HEADS, 128), f32),
            ],
        ),
        compiler_params=params(40),
        cost_estimate=cost(2 * ROWS * HEADS * LEN * 1088, 6 * MIB, ROWS * HEADS * LEN),
        name="attend_rows",
    )(lengths, rep, own, in_hbm(same), in_hbm(cross), rope, in_hbm(kv))


def on_device(
    query_nope,
    query_rope,
    query_compressed,
    kv_cache,
    cache_lengths,
    key_base,
    query_down,
    query_rise,
    key_down,
    key_rise,
    moe_input,
    expert_ids,
    route_weights,
    expert_gate_up,
):
    rep = lax.axis_index("rep")
    ep_size = lax.axis_size("ep")
    every = [(r, e) for r in range(2) for e in range(ep_size)]
    place = lambda r, e: r * ep_size + e
    to_same = [(place(r, e), place(1 - r, e)) for r, e in every]
    to_cross = [(place(r, e), place(1 - r, e ^ 2)) for r, e in every]
    to_core = [(e, e ^ 1) for e in range(ep_size)]

    factors = (query_rise[0], key_rise[0], key_down[0], query_down[0].T)
    ids = expert_ids.T
    same, cross, mask_a, mask_b = payloads(ids, query_nope, query_compressed, *factors)
    moe_input, same, cross = lax.optimization_barrier((moe_input, same, cross))
    leaving_rows = pack(mask_a, mask_b, moe_input)
    arrived_rows = lax.all_to_all(leaving_rows, AXES, 0, 0, tiled=True)

    from_same = lax.ppermute(same, AXES, to_same)
    from_cross = lax.ppermute(cross, AXES, to_cross)
    half = jnp.concatenate([from_same[:, RISE_Q_AT:], from_cross[:, RISE_Q_AT:]], axis=0)
    other = lax.ppermute(half, "ep", to_core)
    own, same, cross = query_part(
        rep.reshape(1), query_nope, query_compressed, from_same, from_cross, other, *factors, key_base
    )
    same = lax.ppermute(same, AXES, to_same)
    cross = lax.ppermute(cross, AXES, to_cross)
    ids, own = lax.optimization_barrier((ids, own))
    pick_a, pick_b = picks(ids)
    arrived_rows, own, pick_a, pick_b = lax.optimization_barrier(
        (arrived_rows, own, pick_a, pick_b)
    )
    rope = query_rope.reshape(ROWS, HEADS, ROPE)
    activation = expert(arrived_rows, expert_gate_up)
    activation, same, cross = lax.optimization_barrier((activation, same, cross))
    back = lax.all_to_all(activation, AXES, 0, 0, tiled=True)
    attended = attend(cache_lengths, rep.reshape(1), own, same, cross, rope, kv_cache)
    expert_hidden = unpack(pick_a, pick_b, route_weights, back)
    return (attended, expert_hidden)


def solution(mesh):
    both = ("rep", "ep")
    return jax.shard_map(
        on_device,
        mesh=mesh,
        in_specs=(
            P(both, None),
            P(both, None),
            P(both, None),
            P(both, None, None),
            P(both),
            P("rep", None, None),
            P("rep", None, None),
            P("rep", None, None),
            P("rep", None, None),
            P("rep", None, None),
            P(both, None),
            P(both, None),
            P(both, None),
            P(both, None, None),
        ),
        out_specs=(P(both, None), P(both, None)),
        check_vma=False,
    )
```
